32 devices in a mesh: sub: 4 (over y, x), frow: 4 (over z), fcol: 2 (over core).
Axes of the slice: x: 2, y: 2, z: 4, core: 2. Of those that a mesh axis runs over, the one named last changes fastest.
Arguments:
- subgrids: float32 [128, 2, 512, 512], P('sub', None, ('frow', 'fcol')), may hold values from -0.01171875 to 0.01171875
- window: float32 [512, 512], P(('frow', 'fcol')), may hold values from 0.25 to 1
- counts: int32 [4], P('sub'), may hold values from 1 to 32, as said below
- nonempty: int32 [128], P('sub'), may hold values from -1 to 127, as said below
- column_u: int32 [1], replicated, may hold values from 0 to 65535
Outputs:
- facets: float32 [8, 2, 512, 8192], P('fcol', None, ('sub', 'frow'))
The draws below stay inside these ranges and needn't reach their ends.
Inputs may be any that keep to these rules, and one draw needn't show every extreme that they name: counts[i] is how many of owner i's 32 slots hold a nonempty subgrid, always its first slots; one owner's count is 32 in every draw. `nonempty`: entries i*32 to (i+1)*32 - 1 belong to owner i; entry i*32+j for j below counts[i] is a distinct column position within i*32 to (i+1)*32 - 1, later entries are -1.
All inputs are finite; a program needn't handle non-finite values.
Results may differ from the reference program's by a relative error of at most 0.0003.
Values sent between devices are 32-bit elements; how exact they have to be, the bound alone decides.
A program may use at most 128 MiB of HBM per device.

```python
import math
import jax
import jax.numpy as jnp
from jax import lax

IMAGE = 65536
FACET = 8192
M = 512
NFAC = 8
POS = 128
CAP = 32
ROWS = 512
N_SUB = 4


def column_plan(key):
    key_count, key_full, key_order = jax.random.split(key, 3)
    owner_counts = jax.random.randint(key_count, (N_SUB,), 1, CAP // 2 + 1)
    full_owner = jax.random.randint(key_full, (), 0, N_SUB)
    owner_counts = jnp.where(jnp.arange(N_SUB) == full_owner, CAP, owner_counts).astype(jnp.int32)
    order_keys = jax.random.split(key_order, N_SUB)
    orders = jax.vmap(lambda single: jax.random.permutation(single, CAP))(order_keys)
    last_order = orders[N_SUB - 1]
    where_last = jnp.argmax((last_order == CAP - 1).astype(jnp.int32))
    first_value = last_order[0]
    last_order = jnp.where(jnp.arange(CAP) == 0, CAP - 1, jnp.where(jnp.arange(CAP) == where_last, first_value, last_order))
    orders = orders.at[N_SUB - 1].set(last_order)
    positions = jnp.arange(N_SUB)[:, None] * CAP + orders
    positions = jnp.where(jnp.arange(CAP)[None, :] < owner_counts[:, None], positions, -1)
    return (owner_counts, positions.reshape(-1).astype(jnp.int32))


def draw_counts(key, part):
    return column_plan(key)[0]


def draw_nonempty(key, part):
    return column_plan(key)[1]


def level_of(rng, dims, pieces, low, top_value):
    level = 1.0
    for dim, blocks in pieces:
        draws = jax.random.uniform(jax.random.fold_in(jax.random.fold_in(rng, 6), dim), (blocks,), jnp.float32, low / len(pieces), top_value / len(pieces))
        level = level * jnp.repeat(jnp.exp(draws), dims[dim] // blocks).reshape((-1,) + (1,) * (len(dims) - 1 - dim))
    return level


def normal_values(rng, shape, deviation, most, cuts=(), held_as=jnp.bfloat16):
    entries = jax.random.normal(rng, shape, jnp.float32) * deviation
    if len(cuts) > 0:
        entries = level_of(rng, shape, cuts, -0.22, 0.18) * entries
    return jnp.clip(entries, min=-most, max=most).astype(held_as)


def setup_inputs(seed: int = 0) -> dict:
    arg_keys = jax.random.split(jax.random.key(seed), 6)
    subgrids = normal_values(arg_keys[0], (POS, 2, M, M), (1.0 / M), 0.01171875, ((0, 4), (2, 8)), jnp.float32)
    window = jnp.clip(0.25 + 0.75 * jax.random.uniform(arg_keys[1], (M, M), jnp.float32) ** level_of(arg_keys[1], (M, M), ((0, 8),), -0.2, 0.2), 0.25, 1.0)
    counts = draw_counts(jax.random.fold_in(arg_keys[5], 71), 0)
    nonempty = draw_nonempty(jax.random.fold_in(arg_keys[5], 71), 0)
    column_u = jax.random.randint(arg_keys[4], (1,), 0, IMAGE).astype(jnp.int32)
    return dict(subgrids=subgrids, window=window, counts=counts, nonempty=nonempty, column_u=column_u)


def twiddles(index):
    angle = index.astype(jnp.float32) * (2.0 * math.pi / IMAGE)
    return jnp.cos(angle), jnp.sin(angle)


def reference(subgrids, window, counts, nonempty, column_u):
    highest = lax.Precision.HIGHEST
    alive = (jnp.arange(CAP, dtype=jnp.int32)[None, :] < counts[:, None]).reshape(-1)
    row_ids = jnp.arange(ROWS, dtype=jnp.int32)

    def add_slot(running, item):
        slot_data, position, keep = item
        weighted = slot_data * window[None]
        v_ids = jnp.arange(M, dtype=jnp.int32) + jnp.maximum(position, 0) * M
        cos_part, sin_part = twiddles((row_ids[:, None] * v_ids[None, :]) % IMAGE)
        real_part = jnp.dot(cos_part, weighted[0], precision=highest, preferred_element_type=jnp.float32) - jnp.dot(sin_part, weighted[1], precision=highest, preferred_element_type=jnp.float32)
        imag_part = jnp.dot(sin_part, weighted[0], precision=highest, preferred_element_type=jnp.float32) + jnp.dot(cos_part, weighted[1], precision=highest, preferred_element_type=jnp.float32)
        term = jnp.stack([real_part, imag_part])
        return running + jnp.where(keep, term, jnp.zeros_like(term)), None

    column_sum, _ = lax.scan(add_slot, jnp.zeros((2, ROWS, M), jnp.float32), (subgrids, nonempty, alive))
    u_ids = (jnp.arange(M, dtype=jnp.int32) + column_u[0]) % IMAGE
    base_ids = (FACET * u_ids) % IMAGE
    cos_col, sin_col = twiddles((u_ids[:, None] * jnp.arange(FACET, dtype=jnp.int32)[None, :]) % IMAGE)

    def one_facet(facet_id):
        cos_facet, sin_facet = twiddles((facet_id * base_ids) % IMAGE)
        rot_real = column_sum[0] * cos_facet[None, :] - column_sum[1] * sin_facet[None, :]
        rot_imag = column_sum[0] * sin_facet[None, :] + column_sum[1] * cos_facet[None, :]
        out_real = jnp.dot(rot_real, cos_col, precision=highest, preferred_element_type=jnp.float32) - jnp.dot(rot_imag, sin_col, precision=highest, preferred_element_type=jnp.float32)
        out_imag = jnp.dot(rot_real, sin_col, precision=highest, preferred_element_type=jnp.float32) + jnp.dot(rot_imag, cos_col, precision=highest, preferred_element_type=jnp.float32)
        return jnp.stack([out_real, out_imag])

    return lax.map(one_facet, jnp.arange(NFAC, dtype=jnp.int32))
```

```python
import functools
import math

import jax
import jax.numpy as jnp
from jax import lax
from jax.experimental import pallas as pl
from jax.experimental.pallas import tpu as pltpu
from jax.sharding import PartitionSpec as P

IMAGE = 65536
FACET = 8192
M = 512
ROW_DEV = 32
LANES = 128
VMEM_BYTES = 56 * 1024 * 1024


def sincos(k):
    q = (k + 16384) >> 15
    y = (k - (q << 15)).astype(jnp.float32) * (math.pi / IMAGE)
    z = y * y
    c = 1.0 + z * (-1.0 / 2 + z * (1.0 / 24 + z * (-1.0 / 720 + z * (1.0 / 40320))))
    s = y * (1.0 + z * (-1.0 / 6 + z * (1.0 / 120 + z * (-1.0 / 5040))))
    swap = (q & 1) == 1
    cos_part = jnp.where(swap, s, c)
    sin_part = jnp.where(swap, c, s)
    cos_part = jnp.where(((q + 1) & 2) != 0, -cos_part, cos_part)
    sin_part = jnp.where((q & 2) != 0, -sin_part, sin_part)
    return cos_part, sin_part


def split(x):
    high = x.astype(jnp.bfloat16)
    low = (x - high.astype(jnp.float32)).astype(jnp.bfloat16)
    return high, low


def column_kernel(group, start_ref, count_ref, pos_ref, sub_ref, win_ref, out_ref, left, rot, xs, acc):
    cap, _, v_count, _ = sub_ref.shape
    rows = out_ref.shape[1]
    half = rows // 2
    depth = group * v_count
    n_groups = (count_ref[0] + group - 1) // group

    @pl.when(pl.program_id(0) == 0)
    def _():
        def one_slot(slot, carry):
            v = lax.broadcasted_iota(jnp.int32, (v_count, LANES), 0) + start_ref[0]
            n = v + M * jnp.maximum(pos_ref[slot], 0)
            cos_part, sin_part = sincos((rows - 1) * n)
            live = jnp.where(slot < count_ref[0], 1.0, 0.0)
            rot[slot, 0] = cos_part * live
            rot[slot, 1] = sin_part * live
            return carry

        lax.fori_loop(0, n_groups * group, one_slot, 0)
        step = 32

        def one_block(item, carry):
            g = item // (half // step)
            r = item % (half // step)
            lane = lax.broadcasted_iota(jnp.int32, (1, depth), 1)
            slot_of = lane // v_count
            p = jnp.zeros((1, depth), jnp.int32)
            for s in range(group):
                p = jnp.where(slot_of == s, jnp.maximum(pos_ref[g * group + s], 0), p)
            n = lane % v_count + start_ref[0] + M * p
            d = lax.broadcasted_iota(jnp.int32, (step, 1), 0) + r * step
            cos_part, sin_part = sincos((2 * d + 1) * n)
            for part, base in ((cos_part, 0), (sin_part, half)):
                high, low = split(part)
                here = pl.ds(pl.multiple_of(base + r * step, step), step)
                left[g, here, 0:depth] = high
                left[g, here, depth : 2 * depth] = low
                left[g, here, 2 * depth : 3 * depth] = high
            return carry

        lax.fori_loop(0, n_groups * (half // step), one_block, 0)

    acc[...] = jnp.zeros_like(acc)

    def one_group(g, carry):
        for s in range(group):
            slot = g * group + s
            wc = win_ref[...] * rot[slot, 0]
            ws = win_ref[...] * rot[slot, 1]
            xr, xi = sub_ref[slot, 0], sub_ref[slot, 1]
            x = jnp.concatenate([xr * wc - xi * ws, xr * ws + xi * wc], 1)
            high, low = split(x)
            xs[s * v_count : (s + 1) * v_count, :] = high
            xs[depth + s * v_count : depth + (s + 1) * v_count, :] = low
        high = xs[0:depth, :]
        right = jnp.concatenate([high, high, xs[depth : 2 * depth, :]], 0)
        acc[...] += jnp.dot(left[g], right, preferred_element_type=jnp.float32)
        return carry

    lax.fori_loop(0, n_groups, one_group, 0)
    n_low = half // ROW_DEV
    for k in range(n_low):
        d = slice(k * ROW_DEV, (k + 1) * ROW_DEV)
        e = slice(half + k * ROW_DEV, half + (k + 1) * ROW_DEV)
        cr, ci = acc[d, :LANES], acc[d, LANES:]
        sr, si = acc[e, :LANES], acc[e, LANES:]
        out_ref[0, e, :] = cr - si
        out_ref[1, e, :] = sr + ci
        lower = slice((n_low - 1 - k) * ROW_DEV, (n_low - k) * ROW_DEV)
        out_ref[0, lower, :] = cr + si
        out_ref[1, lower, :] = ci - sr


def column_partial(subgrids, window, counts, nonempty, v_start, rows):
    cap, _, v_count, width = subgrids.shape
    group = min(8, cap)
    depth = group * v_count
    flops = 2 * rows * 2 * width * cap * v_count * 3
    return pl.pallas_call(
        functools.partial(column_kernel, group),
        grid=(width // LANES,),
        out_shape=jax.ShapeDtypeStruct((2, rows, width), jnp.float32),
        in_specs=[
            pl.BlockSpec(memory_space=pltpu.SMEM),
            pl.BlockSpec(memory_space=pltpu.SMEM),
            pl.BlockSpec(memory_space=pltpu.SMEM),
            pl.BlockSpec((cap, 2, v_count, LANES), lambda t: (0, 0, 0, t)),
            pl.BlockSpec((v_count, LANES), lambda t: (0, t)),
        ],
        out_specs=pl.BlockSpec((2, rows, LANES), lambda t: (0, 0, t)),
        scratch_shapes=[
            pltpu.VMEM((cap // group, rows, 3 * depth), jnp.bfloat16),
            pltpu.VMEM((cap, 2, v_count, LANES), jnp.float32),
            pltpu.VMEM((2 * depth, 2 * LANES), jnp.bfloat16),
            pltpu.VMEM((rows, 2 * LANES), jnp.float32),
        ],
        compiler_params=pltpu.CompilerParams(vmem_limit_bytes=VMEM_BYTES),
        cost_estimate=pl.CostEstimate(flops=flops, bytes_accessed=12 << 20, transcendentals=0),
        name="column_sum",
    )(v_start, counts, nonempty, subgrids, window)


TILE = 512


def reverse_lanes(x):
    index = (LANES - 1) - lax.broadcasted_iota(jnp.int32, (x.shape[0], LANES), 1)
    n = x.shape[1] // LANES
    parts = [
        jnp.take_along_axis(x[:, (n - 1 - i) * LANES : (n - i) * LANES], index, axis=1)
        for i in range(n)
    ]
    return jnp.concatenate(parts, 1)


def facet_kernel(n_local, meta_ref, sum_ref, out_ref, left, base, right, buf, sem):
    t = pl.program_id(0)
    steps = pl.num_programs(0)
    column = meta_ref[0]
    first = meta_ref[1]
    rows = sum_ref.shape[1]
    mid = FACET // 2

    @pl.when(t == 0)
    def _():
        u = lax.broadcasted_iota(jnp.int32, (1, M), 1)
        w = (u + column) & (IMAGE - 1)
        for j in range(n_local):
            cos_part, sin_part = sincos((2 * FACET * (first + j) + FACET - 1) * w)
            re, im = sum_ref[0], sum_ref[1]
            for part, value in ((0, re * cos_part - im * sin_part), (1, re * sin_part + im * cos_part)):
                high, low = split(value)
                here = slice((2 * j + part) * rows, (2 * j + part + 1) * rows)
                left[here, 0:M] = high
                left[here, M : 2 * M] = low
                left[here, 2 * M : 3 * M] = high

        def one_block(i, carry):
            here = pl.ds(pl.multiple_of(i * 16, 16), 16)
            w = (lax.broadcasted_iota(jnp.int32, (16, 1), 0) + i * 16 + column) & (IMAGE - 1)
            d = lax.broadcasted_iota(jnp.int32, (1, TILE), 1)
            cos_part, sin_part = sincos((2 * d + 1) * w)
            base[0, here, :] = cos_part
            base[1, here, :] = sin_part
            return carry

        lax.fori_loop(0, M // 16, one_block, 0)

    def one_block(i, carry):
        here = pl.ds(pl.multiple_of(i * 16, 16), 16)
        low_here = pl.ds(pl.multiple_of(M + i * 16, 16), 16)
        w = (lax.broadcasted_iota(jnp.int32, (16, LANES), 0) + i * 16 + column) & (IMAGE - 1)
        tc, ts = sincos((2 * TILE * t) * w)
        for k in range(TILE // LANES):
            lanes = slice(k * LANES, (k + 1) * LANES)
            bc, bs = base[0, here, lanes], base[1, here, lanes]
            high, low = split(bc * tc - bs * ts)
            right[here, lanes] = high
            right[low_here, lanes] = low
            lanes = slice(TILE + k * LANES, TILE + (k + 1) * LANES)
            high, low = split(bc * ts + bs * tc)
            right[here, lanes] = high
            right[low_here, lanes] = low
        return carry

    lax.fori_loop(0, M // 16, one_block, 0, unroll=2)
    slot = lax.rem(t, 2)

    def copies(step, place):
        upper = pltpu.make_async_copy(
            buf.at[place, 0],
            out_ref.at[:, :, :, pl.ds(pl.multiple_of(mid + step * TILE, TILE), TILE)],
            sem.at[place, 0],
        )
        lower = pltpu.make_async_copy(
            buf.at[place, 1],
            out_ref.at[:, :, :, pl.ds(pl.multiple_of(mid - (step + 1) * TILE, TILE), TILE)],
            sem.at[place, 1],
        )
        return upper, lower

    @pl.when(t >= 2)
    def _():
        for copy in copies(t - 2, slot):
            copy.wait()

    high = right[0:M, :]
    both = jnp.concatenate([high, high, right[M : 2 * M, :]], 0)
    for j in range(n_local):
        here = slice(2 * j * rows, 2 * (j + 1) * rows)
        product = jnp.dot(left[here, :], both, preferred_element_type=jnp.float32)
        rc, rs = product[:rows, :TILE], product[:rows, TILE:]
        ic, is_ = product[rows:, :TILE], product[rows:, TILE:]
        buf[slot, 0, j, 0] = rc - is_
        buf[slot, 0, j, 1] = rs + ic
        buf[slot, 1, j, 0] = reverse_lanes(rc + is_)
        buf[slot, 1, j, 1] = reverse_lanes(ic - rs)
    for copy in copies(t, slot):
        copy.start()

    @pl.when(t == steps - 1)
    def _():
        for copy in copies(t - 1, 1 - slot):
            copy.wait()
        for copy in copies(t, slot):
            copy.wait()


def facet_rows(column_sum, meta, n_local):
    rows = column_sum.shape[1]
    flops = 2 * (2 * n_local * rows) * (3 * M) * FACET
    return pl.pallas_call(
        functools.partial(facet_kernel, n_local),
        grid=(FACET // 2 // TILE,),
        out_shape=jax.ShapeDtypeStruct((n_local, 2, rows, FACET), jnp.float32),
        in_specs=[
            pl.BlockSpec(memory_space=pltpu.SMEM),
            pl.BlockSpec((2, rows, M), lambda t: (0, 0, 0)),
        ],
        out_specs=pl.BlockSpec(memory_space=pl.ANY),
        scratch_shapes=[
            pltpu.VMEM((2 * n_local * rows, 3 * M), jnp.bfloat16),
            pltpu.VMEM((2, M, TILE), jnp.float32),
            pltpu.VMEM((2 * M, 2 * TILE), jnp.bfloat16),
            pltpu.VMEM((2, 2, n_local, 2, rows, TILE), jnp.float32),
            pltpu.SemaphoreType.DMA((2, 2)),
        ],
        compiler_params=pltpu.CompilerParams(vmem_limit_bytes=VMEM_BYTES),
        cost_estimate=pl.CostEstimate(flops=flops, bytes_accessed=9 << 20, transcendentals=0),
        name="facet_rows",
    )(meta, column_sum)


def local(subgrids, window, counts, nonempty, column_u):
    n_blocks = lax.axis_size("sub") * lax.axis_size("frow")
    rows = ROW_DEV * n_blocks
    v_start = lax.axis_index(("frow", "fcol")) * subgrids.shape[2]
    partial_sum = column_partial(
        subgrids, window, counts, nonempty, v_start.astype(jnp.int32).reshape(1), rows
    )
    own_rows = lax.psum_scatter(
        partial_sum, ("sub", "frow", "fcol"), scatter_dimension=1, tiled=True
    )
    pair_sum = lax.all_gather(own_rows, "fcol", axis=1, tiled=True)
    block = lax.axis_index(("sub", "frow"))
    pair_sum = jnp.where(block < n_blocks // 2, jnp.flip(pair_sum, 1), pair_sum)
    n_local = IMAGE // FACET // lax.axis_size("fcol")
    meta = jnp.stack([column_u[0], (lax.axis_index("fcol") * n_local).astype(jnp.int32)])
    return facet_rows(pair_sum, meta, n_local)


def solution(mesh):
    return jax.shard_map(
        local,
        mesh=mesh,
        in_specs=(
            P("sub", None, ("frow", "fcol"), None),
            P(("frow", "fcol"), None),
            P("sub"),
            P("sub"),
            P(),
        ),
        out_specs=P("fcol", None, ("sub", "frow"), None),
        check_vma=False,
    )
```

```python
import functools
import math

import jax
import jax.numpy as jnp
from jax import lax
from jax.experimental import pallas as pl
from jax.experimental.pallas import tpu as pltpu
from jax.sharding import PartitionSpec as P

IMAGE = 65536
FACET = 8192
M = 512
ROW_DEV = 32
LANES = 128
VMEM_BYTES = 56 * 1024 * 1024


def sincos(k):
    q = (k + 16384) >> 15
    y = (k - (q << 15)).astype(jnp.float32) * (math.pi / IMAGE)
    z = y * y
    c = 1.0 + z * (-1.0 / 2 + z * (1.0 / 24 + z * (-1.0 / 720 + z * (1.0 / 40320))))
    s = y * (1.0 + z * (-1.0 / 6 + z * (1.0 / 120 + z * (-1.0 / 5040))))
    swap = (q & 1) == 1
    cos_part = jnp.where(swap, s, c)
    sin_part = jnp.where(swap, c, s)
    cos_part = jnp.where(((q + 1) & 2) != 0, -cos_part, cos_part)
    sin_part = jnp.where((q & 2) != 0, -sin_part, sin_part)
    return cos_part, sin_part


def split(x):
    high = x.astype(jnp.bfloat16)
    low = (x - high.astype(jnp.float32)).astype(jnp.bfloat16)
    return high, low


def column_kernel(group, start_ref, count_ref, pos_ref, sub_ref, win_ref, out_ref, left, rot, xs, acc):
    cap, _, v_count, _ = sub_ref.shape
    rows = out_ref.shape[2]
    half = rows // 2
    depth = group * v_count
    n_groups = (count_ref[0] + group - 1) // group

    @pl.when(pl.program_id(0) == 0)
    def _():
        def one_slot(slot, carry):
            v = lax.broadcasted_iota(jnp.int32, (v_count, LANES), 0) + start_ref[0]
            n = v + M * jnp.maximum(pos_ref[slot], 0)
            cos_part, sin_part = sincos((rows - 1) * n)
            live = jnp.where(slot < count_ref[0], 1.0, 0.0)
            rot[slot, 0] = cos_part * live
            rot[slot, 1] = sin_part * live
            return carry

        lax.fori_loop(0, n_groups * group, one_slot, 0)
        step = 32

        def one_block(item, carry):
            g = item // (half // step)
            r = item % (half // step)
            lane = lax.broadcasted_iota(jnp.int32, (1, depth), 1)
            slot_of = lane // v_count
            p = jnp.zeros((1, depth), jnp.int32)
            for s in range(group):
                p = jnp.where(slot_of == s, jnp.maximum(pos_ref[g * group + s], 0), p)
            n = lane % v_count + start_ref[0] + M * p
            d = lax.broadcasted_iota(jnp.int32, (step, 1), 0) + r * step
            cos_part, sin_part = sincos((2 * d + 1) * n)
            for part, base in ((cos_part, 0), (sin_part, half)):
                high, low = split(part)
                here = pl.ds(pl.multiple_of(base + r * step, step), step)
                left[g, here, 0:depth] = high
                left[g, here, depth : 2 * depth] = low
                left[g, here, 2 * depth : 3 * depth] = high
            return carry

        lax.fori_loop(0, n_groups * (half // step), one_block, 0)

    acc[...] = jnp.zeros_like(acc)

    def one_group(g, carry):
        for s in range(group):
            slot = g * group + s
            wc = win_ref[...] * rot[slot, 0]
            ws = win_ref[...] * rot[slot, 1]
            xr, xi = sub_ref[slot, 0], sub_ref[slot, 1]
            x = jnp.concatenate([xr * wc - xi * ws, xr * ws + xi * wc], 1)
            high, low = split(x)
            xs[s * v_count : (s + 1) * v_count, :] = high
            xs[depth + s * v_count : depth + (s + 1) * v_count, :] = low
        high = xs[0:depth, :]
        right = jnp.concatenate([high, high, xs[depth : 2 * depth, :]], 0)
        acc[...] += jnp.dot(left[g], right, preferred_element_type=jnp.float32)
        return carry

    lax.fori_loop(0, n_groups, one_group, 0)
    n_low = half // ROW_DEV
    for k in range(n_low):
        d = slice(k * ROW_DEV, (k + 1) * ROW_DEV)
        e = slice(half + k * ROW_DEV, half + (k + 1) * ROW_DEV)
        cr, ci = acc[d, :LANES], acc[d, LANES:]
        sr, si = acc[e, :LANES], acc[e, LANES:]
        out_ref[0, 0, e, :] = cr - si
        out_ref[0, 1, e, :] = sr + ci
        lower = slice((n_low - 1 - k) * ROW_DEV, (n_low - k) * ROW_DEV)
        out_ref[0, 0, lower, :] = cr + si
        out_ref[0, 1, lower, :] = ci - sr


def column_partial(subgrids, window, counts, nonempty, v_start, rows):
    cap, _, v_count, width = subgrids.shape
    group = min(8, cap)
    depth = group * v_count
    flops = 2 * rows * 2 * width * cap * v_count * 3
    return pl.pallas_call(
        functools.partial(column_kernel, group),
        grid=(width // LANES,),
        out_shape=jax.ShapeDtypeStruct((width // LANES, 2, rows, LANES), jnp.float32),
        in_specs=[
            pl.BlockSpec(memory_space=pltpu.SMEM),
            pl.BlockSpec(memory_space=pltpu.SMEM),
            pl.BlockSpec(memory_space=pltpu.SMEM),
            pl.BlockSpec((cap, 2, v_count, LANES), lambda t: (0, 0, 0, t)),
            pl.BlockSpec((v_count, LANES), lambda t: (0, t)),
        ],
        out_specs=pl.BlockSpec((1, 2, rows, LANES), lambda t: (t, 0, 0, 0)),
        scratch_shapes=[
            pltpu.VMEM((cap // group, rows, 3 * depth), jnp.bfloat16),
            pltpu.VMEM((cap, 2, v_count, LANES), jnp.float32),
            pltpu.VMEM((2 * depth, 2 * LANES), jnp.bfloat16),
            pltpu.VMEM((rows, 2 * LANES), jnp.float32),
        ],
        compiler_params=pltpu.CompilerParams(vmem_limit_bytes=VMEM_BYTES),
        cost_estimate=pl.CostEstimate(flops=flops, bytes_accessed=12 << 20, transcendentals=0),
        name="column_sum",
    )(v_start, counts, nonempty, subgrids, window)


TILE = 512


def reverse_lanes(x):
    index = (LANES - 1) - lax.broadcasted_iota(jnp.int32, (x.shape[0], LANES), 1)
    n = x.shape[1] // LANES
    parts = [
        jnp.take_along_axis(x[:, (n - 1 - i) * LANES : (n - i) * LANES], index, axis=1)
        for i in range(n)
    ]
    return jnp.concatenate(parts, 1)


def facet_kernel(n_local, meta_ref, sum_ref, out_ref, left, base, right, buf, sem):
    t = pl.program_id(0)
    steps = pl.num_programs(0)
    column = meta_ref[0]
    first = meta_ref[1]
    rows = sum_ref.shape[1]
    mid = FACET // 2

    @pl.when(t == 0)
    def _():
        u = lax.broadcasted_iota(jnp.int32, (1, M), 1)
        w = (u + column) & (IMAGE - 1)
        for j in range(n_local):
            cos_part, sin_part = sincos((2 * FACET * (first + j) + FACET - 1) * w)
            re, im = sum_ref[0], sum_ref[1]
            for part, value in ((0, re * cos_part - im * sin_part), (1, re * sin_part + im * cos_part)):
                high, low = split(value)
                here = slice((2 * j + part) * rows, (2 * j + part + 1) * rows)
                left[here, 0:M] = high
                left[here, M : 2 * M] = low
                left[here, 2 * M : 3 * M] = high

        def one_block(i, carry):
            here = pl.ds(pl.multiple_of(i * 16, 16), 16)
            w = (lax.broadcasted_iota(jnp.int32, (16, 1), 0) + i * 16 + column) & (IMAGE - 1)
            d = lax.broadcasted_iota(jnp.int32, (1, TILE), 1)
            cos_part, sin_part = sincos((2 * d + 1) * w)
            base[0, here, :] = cos_part
            base[1, here, :] = sin_part
            return carry

        lax.fori_loop(0, M // 16, one_block, 0)

    def one_block(i, carry):
        here = pl.ds(pl.multiple_of(i * 16, 16), 16)
        low_here = pl.ds(pl.multiple_of(M + i * 16, 16), 16)
        w = (lax.broadcasted_iota(jnp.int32, (16, LANES), 0) + i * 16 + column) & (IMAGE - 1)
        tc, ts = sincos((2 * TILE * t) * w)
        for k in range(TILE // LANES):
            lanes = slice(k * LANES, (k + 1) * LANES)
            bc, bs = base[0, here, lanes], base[1, here, lanes]
            high, low = split(bc * tc - bs * ts)
            right[here, lanes] = high
            right[low_here, lanes] = low
            lanes = slice(TILE + k * LANES, TILE + (k + 1) * LANES)
            high, low = split(bc * ts + bs * tc)
            right[here, lanes] = high
            right[low_here, lanes] = low
        return carry

    lax.fori_loop(0, M // 16, one_block, 0, unroll=2)
    slot = lax.rem(t, 2)

    def copies(step, place):
        upper = pltpu.make_async_copy(
            buf.at[place, 0],
            out_ref.at[:, :, :, pl.ds(pl.multiple_of(mid + step * TILE, TILE), TILE)],
            sem.at[place, 0],
        )
        lower = pltpu.make_async_copy(
            buf.at[place, 1],
            out_ref.at[:, :, :, pl.ds(pl.multiple_of(mid - (step + 1) * TILE, TILE), TILE)],
            sem.at[place, 1],
        )
        return upper, lower

    @pl.when(t >= 2)
    def _():
        for copy in copies(t - 2, slot):
            copy.wait()

    high = right[0:M, :]
    both = jnp.concatenate([high, high, right[M : 2 * M, :]], 0)
    products = jnp.dot(left[...], both, preferred_element_type=jnp.float32)
    for j in range(n_local):
        product = products[2 * j * rows : 2 * (j + 1) * rows]
        rc, rs = product[:rows, :TILE], product[:rows, TILE:]
        ic, is_ = product[rows:, :TILE], product[rows:, TILE:]
        buf[slot, 0, j, 0] = rc - is_
        buf[slot, 0, j, 1] = rs + ic
        buf[slot, 1, j, 0] = reverse_lanes(rc + is_)
        buf[slot, 1, j, 1] = reverse_lanes(ic - rs)
    for copy in copies(t, slot):
        copy.start()

    @pl.when(t == steps - 1)
    def _():
        for copy in copies(t - 1, 1 - slot):
            copy.wait()
        for copy in copies(t, slot):
            copy.wait()


def facet_rows(column_sum, meta, n_local):
    rows = column_sum.shape[1]
    flops = 2 * (2 * n_local * rows) * (3 * M) * FACET
    return pl.pallas_call(
        functools.partial(facet_kernel, n_local),
        grid=(FACET // 2 // TILE,),
        out_shape=jax.ShapeDtypeStruct((n_local, 2, rows, FACET), jnp.float32),
        in_specs=[
            pl.BlockSpec(memory_space=pltpu.SMEM),
            pl.BlockSpec((2, rows, M), lambda t: (0, 0, 0)),
        ],
        out_specs=pl.BlockSpec(memory_space=pl.ANY),
        scratch_shapes=[
            pltpu.VMEM((2 * n_local * rows, 3 * M), jnp.bfloat16),
            pltpu.VMEM((2, M, TILE), jnp.float32),
            pltpu.VMEM((2 * M, 2 * TILE), jnp.bfloat16),
            pltpu.VMEM((2, 2, n_local, 2, rows, TILE), jnp.float32),
            pltpu.SemaphoreType.DMA((2, 2)),
        ],
        compiler_params=pltpu.CompilerParams(vmem_limit_bytes=VMEM_BYTES),
        cost_estimate=pl.CostEstimate(flops=flops, bytes_accessed=9 << 20, transcendentals=0),
        name="facet_rows",
    )(meta, column_sum)


def sum_kernel(sizes, x_ref, out_ref, half_in, half_sum, sub_in, sub_sum, row_in, row_sum, pair_in, *sems):
    n_sub, n_row, n_chunk = sizes
    sub, row, col = lax.axis_index("sub"), lax.axis_index("frow"), lax.axis_index("fcol")
    partner = 1 - col
    barrier = pltpu.get_barrier_semaphore()
    targets = [{"fcol": partner}]
    targets += [{"sub": lax.rem(sub + k, n_sub)} for k in range(1, n_sub)]
    targets += [{"frow": lax.rem(row + k, n_row)} for k in range(1, n_row)]
    for target in targets:
        pl.semaphore_signal(barrier, inc=1, device_id=target, device_id_type=pl.DeviceIdType.MESH)
    pl.semaphore_wait(barrier, len(targets))
    half_send, half_recv, sub_send, sub_recv, row_send, row_recv, pair_send, pair_recv = sems
    sub_rows = half_sum.shape[2] // n_sub

    def copy(src, dst, send, recv, target):
        return pltpu.make_async_remote_copy(
            src_ref=src, dst_ref=dst, send_sem=send, recv_sem=recv,
            device_id=target, device_id_type=pl.DeviceIdType.MESH,
        )

    started = []
    halves = [
        copy(x_ref.at[partner * n_chunk + q], half_in.at[q], half_send.at[q], half_recv.at[q], {"fcol": partner})
        for q in range(n_chunk)
    ]
    for one in halves:
        one.start()
    started += halves
    subs = []
    for q in range(n_chunk):
        halves[q].wait_recv()
        half_sum[q] = x_ref[col * n_chunk + q] + half_in[q]
        mine = []
        for k in range(1, n_sub):
            other = lax.rem(sub + k, n_sub)
            here = pl.ds(pl.multiple_of(other * sub_rows, sub_rows), sub_rows)
            mine.append(copy(
                half_sum.at[q, :, here, :], sub_in.at[q, k - 1],
                sub_send.at[q, k - 1], sub_recv.at[q, k - 1], {"sub": other},
            ))
        for one in mine:
            one.start()
        subs.append(mine)
        started += mine
    rows_sent = []
    for q in range(n_chunk):
        own = pl.ds(pl.multiple_of(sub * sub_rows, sub_rows), sub_rows)
        total = half_sum[q, :, own, :]
        for k in range(1, n_sub):
            subs[q][k - 1].wait_recv()
            total = total + sub_in[q, k - 1]
        sub_sum[q] = total
        mine = []
        for k in range(1, n_row):
            other = lax.rem(row + k, n_row)
            here = pl.ds(pl.multiple_of(other * ROW_DEV, ROW_DEV), ROW_DEV)
            mine.append(copy(
                sub_sum.at[q, :, here, :], row_in.at[q, k - 1],
                row_send.at[q, k - 1], row_recv.at[q, k - 1], {"frow": other},
            ))
        for one in mine:
            one.start()
        rows_sent.append(mine)
        started += mine
    pairs = []
    for q in range(n_chunk):
        own = pl.ds(pl.multiple_of(row * ROW_DEV, ROW_DEV), ROW_DEV)
        total = sub_sum[q, :, own, :]
        for k in range(1, n_row):
            rows_sent[q][k - 1].wait_recv()
            total = total + row_in[q, k - 1]
        row_sum[q] = total
        out_ref[col * n_chunk + q] = total
        one = copy(row_sum.at[q], pair_in.at[q], pair_send.at[q], pair_recv.at[q], {"fcol": partner})
        one.start()
        pairs.append(one)
    started += pairs
    for q in range(n_chunk):
        pairs[q].wait_recv()
        out_ref[partner * n_chunk + q] = pair_in[q]
    for one in started:
        one.wait_send()


def sum_rows(partial_sum):
    chunks, _, rows, lanes = partial_sum.shape
    n_sub, n_row = lax.axis_size("sub"), lax.axis_size("frow")
    q = chunks // 2
    f32 = jnp.float32
    dma = pltpu.SemaphoreType.DMA
    return pl.pallas_call(
        functools.partial(sum_kernel, (n_sub, n_row, q)),
        out_shape=jax.ShapeDtypeStruct((chunks, 2, ROW_DEV, lanes), f32),
        in_specs=[pl.BlockSpec(memory_space=pltpu.VMEM)],
        out_specs=pl.BlockSpec(memory_space=pltpu.VMEM),
        scratch_shapes=[
            pltpu.VMEM((q, 2, rows, lanes), f32),
            pltpu.VMEM((q, 2, rows, lanes), f32),
            pltpu.VMEM((q, n_sub - 1, 2, rows // n_sub, lanes), f32),
            pltpu.VMEM((q, 2, rows // n_sub, lanes), f32),
            pltpu.VMEM((q, n_row - 1, 2, ROW_DEV, lanes), f32),
            pltpu.VMEM((q, 2, ROW_DEV, lanes), f32),
            pltpu.VMEM((q, 2, ROW_DEV, lanes), f32),
            dma((q,)), dma((q,)),
            dma((q, n_sub - 1)), dma((q, n_sub - 1)),
            dma((q, n_row - 1)), dma((q, n_row - 1)),
            dma((q,)), dma((q,)),
        ],
        compiler_params=pltpu.CompilerParams(
            collective_id=0, has_side_effects=True, vmem_limit_bytes=VMEM_BYTES
        ),
        name="sum_rows",
    )(partial_sum)


def local(subgrids, window, counts, nonempty, column_u):
    n_blocks = lax.axis_size("sub") * lax.axis_size("frow")
    rows = ROW_DEV * n_blocks
    v_start = lax.axis_index(("frow", "fcol")) * subgrids.shape[2]
    partial_sum = column_partial(
        subgrids, window, counts, nonempty, v_start.astype(jnp.int32).reshape(1), rows
    )
    chunks = sum_rows(partial_sum)
    pair_sum = chunks.transpose(1, 2, 0, 3).reshape(2, ROW_DEV, chunks.shape[0] * LANES)
    block = lax.axis_index(("sub", "frow"))
    pair_sum = jnp.where(block < n_blocks // 2, jnp.flip(pair_sum, 1), pair_sum)
    n_local = IMAGE // FACET // lax.axis_size("fcol")
    meta = jnp.stack([column_u[0], (lax.axis_index("fcol") * n_local).astype(jnp.int32)])
    return facet_rows(pair_sum, meta, n_local)


def solution(mesh):
    return jax.shard_map(
        local,
        mesh=mesh,
        in_specs=(
            P("sub", None, ("frow", "fcol"), None),
            P(("frow", "fcol"), None),
            P("sub"),
            P("sub"),
            P(),
        ),
        out_specs=P("fcol", None, ("sub", "frow"), None),
        check_vma=False,
    )
```

```python
import functools
import math

import jax
import jax.numpy as jnp
from jax import lax
from jax.experimental import pallas as pl
from jax.experimental.pallas import tpu as pltpu
from jax.sharding import PartitionSpec as P

IMAGE = 65536
FACET = 8192
M = 512
ROW_DEV = 32
LANES = 128
VMEM_BYTES = 56 * 1024 * 1024


def sincos(k):
    q = (k + 16384) >> 15
    y = (k - (q << 15)).astype(jnp.float32) * (math.pi / IMAGE)
    z = y * y
    c = 1.0 + z * (-1.0 / 2 + z * (1.0 / 24 + z * (-1.0 / 720 + z * (1.0 / 40320))))
    s = y * (1.0 + z * (-1.0 / 6 + z * (1.0 / 120 + z * (-1.0 / 5040))))
    swap = (q & 1) == 1
    cos_part = jnp.where(swap, s, c)
    sin_part = jnp.where(swap, c, s)
    cos_part = jnp.where(((q + 1) & 2) != 0, -cos_part, cos_part)
    sin_part = jnp.where((q & 2) != 0, -sin_part, sin_part)
    return cos_part, sin_part


def split(x):
    high = x.astype(jnp.bfloat16)
    low = (x - high.astype(jnp.float32)).astype(jnp.bfloat16)
    return high, low


def reverse_rows(x):
    index = 7 - lax.broadcasted_iota(jnp.int32, (8, LANES), 0)
    n = x.shape[0] // 8
    parts = [jnp.take_along_axis(x[(n - 1 - i) * 8 : (n - i) * 8], index, axis=0) for i in range(n)]
    return jnp.concatenate(parts, 0)


def column_kernel(group, count_ref, pos_ref, sub_ref, win_ref, out_ref, left, rot, xs_even, xs_odd, acc):
    cap, _, v_count, _ = sub_ref.shape
    rows = out_ref.shape[2]
    half = rows // 2
    depth = group * v_count
    n_pairs = (count_ref[0] + 2 * group - 1) // (2 * group)
    n_groups = 2 * n_pairs
    v_start = (lax.axis_index("frow") * lax.axis_size("fcol") + lax.axis_index("fcol")) * v_count

    @pl.when(pl.program_id(0) == 0)
    def _():
        def one_slot(slot, carry):
            v = lax.broadcasted_iota(jnp.int32, (v_count, LANES), 0) + v_start
            n = v + M * jnp.maximum(pos_ref[slot], 0)
            cos_part, sin_part = sincos((rows - 1) * n)
            live = jnp.where(slot < count_ref[0], 1.0, 0.0)
            rot[slot, 0] = cos_part * live
            rot[slot, 1] = sin_part * live
            return carry

        lax.fori_loop(0, n_groups * group, one_slot, 0)
        step = 32

        def one_block(item, carry):
            g = item // (half // step)
            r = item % (half // step)
            lane = lax.broadcasted_iota(jnp.int32, (1, depth), 1)
            slot_of = lane // v_count
            p = jnp.zeros((1, depth), jnp.int32)
            for s in range(group):
                p = jnp.where(slot_of == s, jnp.maximum(pos_ref[g * group + s], 0), p)
            n = lane % v_count + v_start + M * p
            d = lax.broadcasted_iota(jnp.int32, (step, 1), 0) + r * step
            cos_part, sin_part = sincos((2 * d + 1) * n)
            for part, base in ((cos_part, 0), (sin_part, half)):
                high, low = split(part)
                here = pl.ds(pl.multiple_of(base + r * step, step), step)
                left[g, here, 0:depth] = high
                left[g, here, depth : 2 * depth] = low
                left[g, here, 2 * depth : 3 * depth] = high
            return carry

        lax.fori_loop(0, n_groups * (half // step), one_block, 0)

    acc[...] = jnp.zeros_like(acc)

    def build(g, xs):
        for s in range(group):
            slot = g * group + s
            wc = win_ref[...] * rot[slot, 0]
            ws = win_ref[...] * rot[slot, 1]
            xr, xi = sub_ref[slot, 0], sub_ref[slot, 1]
            x = jnp.concatenate([xr * wc - xi * ws, xr * ws + xi * wc], 1)
            high, low = split(x)
            xs[s * v_count : (s + 1) * v_count, :] = high
            xs[depth + s * v_count : depth + (s + 1) * v_count, :] = low

    def multiply(g, xs):
        high = xs[0:depth, :]
        right = jnp.concatenate([high, high, xs[depth : 2 * depth, :]], 0)
        acc[...] += jnp.dot(left[g], right, preferred_element_type=jnp.float32)

    build(0, xs_even)

    def one_pair(i, carry):
        build(2 * i + 1, xs_odd)
        multiply(2 * i, xs_even)
        build(jnp.minimum(2 * i + 2, n_groups - 1), xs_even)
        multiply(2 * i + 1, xs_odd)
        return carry

    lax.fori_loop(0, n_pairs, one_pair, 0)
    n_low = half // ROW_DEV
    for k in range(n_low):
        d = slice(k * ROW_DEV, (k + 1) * ROW_DEV)
        e = slice(half + k * ROW_DEV, half + (k + 1) * ROW_DEV)
        cr, ci = acc[d, :LANES], acc[d, LANES:]
        sr, si = acc[e, :LANES], acc[e, LANES:]
        out_ref[0, 0, e, :] = cr - si
        out_ref[0, 1, e, :] = sr + ci
        lower = slice((n_low - 1 - k) * ROW_DEV, (n_low - k) * ROW_DEV)
        out_ref[0, 0, lower, :] = reverse_rows(cr + si)
        out_ref[0, 1, lower, :] = reverse_rows(ci - sr)


def column_partial(subgrids, window, counts, nonempty, rows):
    cap, _, v_count, width = subgrids.shape
    group = min(8, cap // 2)
    depth = group * v_count
    flops = 2 * rows * 2 * width * cap * v_count * 3
    return pl.pallas_call(
        functools.partial(column_kernel, group),
        grid=(width // LANES,),
        out_shape=jax.ShapeDtypeStruct((width // LANES, 2, rows, LANES), jnp.float32),
        in_specs=[
            pl.BlockSpec(memory_space=pltpu.SMEM),
            pl.BlockSpec(memory_space=pltpu.SMEM),
            pl.BlockSpec((cap, 2, v_count, LANES), lambda t: (0, 0, 0, t)),
            pl.BlockSpec((v_count, LANES), lambda t: (0, t)),
        ],
        out_specs=pl.BlockSpec((1, 2, rows, LANES), lambda t: (t, 0, 0, 0)),
        scratch_shapes=[
            pltpu.VMEM((cap // group, rows, 3 * depth), jnp.bfloat16),
            pltpu.VMEM((cap, 2, v_count, LANES), jnp.float32),
            pltpu.VMEM((2 * depth, 2 * LANES), jnp.bfloat16),
            pltpu.VMEM((2 * depth, 2 * LANES), jnp.bfloat16),
            pltpu.VMEM((rows, 2 * LANES), jnp.float32),
        ],
        compiler_params=pltpu.CompilerParams(vmem_limit_bytes=VMEM_BYTES),
        cost_estimate=pl.CostEstimate(flops=flops, bytes_accessed=12 << 20, transcendentals=0),
        name="column_sum",
    )(counts, nonempty, subgrids, window)


TILE = 512


def reverse_lanes(x):
    index = (LANES - 1) - lax.broadcasted_iota(jnp.int32, (x.shape[0], LANES), 1)
    n = x.shape[1] // LANES
    parts = [
        jnp.take_along_axis(x[:, (n - 1 - i) * LANES : (n - i) * LANES], index, axis=1)
        for i in range(n)
    ]
    return jnp.concatenate(parts, 1)


def facet_kernel(n_local, column_ref, sum_ref, out_ref, left, base, turn, right, buf, sem):
    t = pl.program_id(0)
    steps = pl.num_programs(0)
    column = column_ref[0]
    first = lax.axis_index("fcol") * n_local
    rows = sum_ref.shape[2]
    chunks = sum_ref.shape[0]
    mid = FACET // 2

    @pl.when(t == 0)
    def _():
        u = lax.broadcasted_iota(jnp.int32, (1, M), 1)
        w = (u + column) & (IMAGE - 1)
        for j in range(n_local):
            cos_part, sin_part = sincos((2 * FACET * (first + j) + FACET - 1) * w)
            re = jnp.concatenate([sum_ref[q, 0] for q in range(chunks)], 1)
            im = jnp.concatenate([sum_ref[q, 1] for q in range(chunks)], 1)
            for part, value in ((0, re * cos_part - im * sin_part), (1, re * sin_part + im * cos_part)):
                high, low = split(value)
                here = slice((2 * j + part) * rows, (2 * j + part + 1) * rows)
                left[here, 0:M] = high
                left[here, M : 2 * M] = low
                left[here, 2 * M : 3 * M] = high

        def one_block(i, carry):
            here = pl.ds(pl.multiple_of(i * 16, 16), 16)
            w = (lax.broadcasted_iota(jnp.int32, (16, 1), 0) + i * 16 + column) & (IMAGE - 1)
            d = lax.broadcasted_iota(jnp.int32, (1, TILE), 1)
            cos_part, sin_part = sincos((2 * d + 1) * w)
            base[0, here, :] = cos_part
            base[1, here, :] = sin_part
            return carry

        lax.fori_loop(0, M // 16, one_block, 0)

    def one_turn(i, carry):
        here = pl.ds(pl.multiple_of(i * 16, 16), 16)
        w = (lax.broadcasted_iota(jnp.int32, (16, LANES), 0) + i * 16 + column) & (IMAGE - 1)
        turn[0, here, :], turn[1, here, :] = sincos((2 * TILE * t) * w)
        return carry

    lax.fori_loop(0, M // 16, one_turn, 0, unroll=4)
    slot = lax.rem(t, 2)

    def copies(step, place):
        upper = pltpu.make_async_copy(
            buf.at[place, 0],
            out_ref.at[:, :, :, pl.ds(pl.multiple_of(mid + step * TILE, TILE), TILE)],
            sem.at[place, 0],
        )
        lower = pltpu.make_async_copy(
            buf.at[place, 1],
            out_ref.at[:, :, :, pl.ds(pl.multiple_of(mid - (step + 1) * TILE, TILE), TILE)],
            sem.at[place, 1],
        )
        return upper, lower

    @pl.when(t >= 2)
    def _():
        for copy in copies(t - 2, slot):
            copy.wait()

    def build(k):
        lanes = slice(k * LANES, (k + 1) * LANES)
        for i in range(M // 16):
            here = slice(i * 16, (i + 1) * 16)
            bc, bs = base[0, here, lanes], base[1, here, lanes]
            tc, ts = turn[0, here, :], turn[1, here, :]
            for part, value in ((0, bc * tc - bs * ts), (1, bc * ts + bs * tc)):
                high, low = split(value)
                place = slice(part * LANES, (part + 1) * LANES)
                right[k, here, place] = high
                right[k, M + i * 16 : M + (i + 1) * 16, place] = low

    n_tiles = TILE // LANES
    build(0)
    for k in range(n_tiles):
        if k + 1 < n_tiles:
            build(k + 1)
        high = right[k, 0:M, :]
        both = jnp.concatenate([high, high, right[k, M : 2 * M, :]], 0)
        products = jnp.dot(left[...], both, preferred_element_type=jnp.float32)
        upper = slice(k * LANES, (k + 1) * LANES)
        lower = slice((n_tiles - 1 - k) * LANES, (n_tiles - k) * LANES)
        for j in range(n_local):
            product = products[2 * j * rows : 2 * (j + 1) * rows]
            rc, rs = product[:rows, :LANES], product[:rows, LANES:]
            ic, is_ = product[rows:, :LANES], product[rows:, LANES:]
            buf[slot, 0, j, 0, :, upper] = rc - is_
            buf[slot, 0, j, 1, :, upper] = rs + ic
            buf[slot, 1, j, 0, :, lower] = reverse_lanes(rc + is_)
            buf[slot, 1, j, 1, :, lower] = reverse_lanes(ic - rs)
    for copy in copies(t, slot):
        copy.start()

    @pl.when(t == steps - 1)
    def _():
        for copy in copies(t - 1, 1 - slot):
            copy.wait()
        for copy in copies(t, slot):
            copy.wait()


def facet_rows(column_sum, column_u, n_local):
    rows = column_sum.shape[2]
    flops = 2 * (2 * n_local * rows) * (3 * M) * FACET
    return pl.pallas_call(
        functools.partial(facet_kernel, n_local),
        grid=(FACET // 2 // TILE,),
        out_shape=jax.ShapeDtypeStruct((n_local, 2, rows, FACET), jnp.float32),
        in_specs=[
            pl.BlockSpec(memory_space=pltpu.SMEM),
            pl.BlockSpec(column_sum.shape, lambda t: (0, 0, 0, 0)),
        ],
        out_specs=pl.BlockSpec(memory_space=pl.ANY),
        scratch_shapes=[
            pltpu.VMEM((2 * n_local * rows, 3 * M), jnp.bfloat16),
            pltpu.VMEM((2, M, TILE), jnp.float32),
            pltpu.VMEM((2, M, LANES), jnp.float32),
            pltpu.VMEM((TILE // LANES, 2 * M, 2 * LANES), jnp.bfloat16),
            pltpu.VMEM((2, 2, n_local, 2, rows, TILE), jnp.float32),
            pltpu.SemaphoreType.DMA((2, 2)),
        ],
        compiler_params=pltpu.CompilerParams(vmem_limit_bytes=VMEM_BYTES),
        cost_estimate=pl.CostEstimate(flops=flops, bytes_accessed=9 << 20, transcendentals=0),
        name="facet_rows",
    )(column_u, column_sum)


def sum_kernel(sizes, x_ref, out_ref, half_in, half_sum, sub_in, sub_sum, row_in, row_sum, pair_in, *sems):
    n_sub, n_row, n_chunk = sizes
    sub, row, col = lax.axis_index("sub"), lax.axis_index("frow"), lax.axis_index("fcol")
    partner = 1 - col
    barrier = pltpu.get_barrier_semaphore()
    targets = [{"fcol": partner}]
    targets += [{"sub": lax.rem(sub + k, n_sub)} for k in range(1, n_sub)]
    targets += [{"frow": lax.rem(row + k, n_row)} for k in range(1, n_row)]
    for target in targets:
        pl.semaphore_signal(barrier, inc=1, device_id=target, device_id_type=pl.DeviceIdType.MESH)
    pl.semaphore_wait(barrier, len(targets))
    half_send, half_recv, sub_send, sub_recv, row_send, row_recv, pair_send, pair_recv = sems
    sub_rows = half_sum.shape[2] // n_sub

    def copy(src, dst, send, recv, target):
        return pltpu.make_async_remote_copy(
            src_ref=src, dst_ref=dst, send_sem=send, recv_sem=recv,
            device_id=target, device_id_type=pl.DeviceIdType.MESH,
        )

    started = []
    halves = [
        copy(x_ref.at[partner * n_chunk + q], half_in.at[q], half_send.at[q], half_recv.at[q], {"fcol": partner})
        for q in range(n_chunk)
    ]
    for one in halves:
        one.start()
    started += halves
    subs = []
    for q in range(n_chunk):
        halves[q].wait_recv()
        half_sum[q] = x_ref[col * n_chunk + q] + half_in[q]
        mine = []
        for k in range(1, n_sub):
            other = lax.rem(sub + k, n_sub)
            here = pl.ds(pl.multiple_of(other * sub_rows, sub_rows), sub_rows)
            mine.append(copy(
                half_sum.at[q, :, here, :], sub_in.at[q, k - 1],
                sub_send.at[q, k - 1], sub_recv.at[q, k - 1], {"sub": other},
            ))
        for one in mine:
            one.start()
        subs.append(mine)
        started += mine
    rows_sent = []
    for q in range(n_chunk):
        own = pl.ds(pl.multiple_of(sub * sub_rows, sub_rows), sub_rows)
        total = half_sum[q, :, own, :]
        for k in range(1, n_sub):
            subs[q][k - 1].wait_recv()
            total = total + sub_in[q, k - 1]
        sub_sum[q] = total
        mine = []
        for k in range(1, n_row):
            other = lax.rem(row + k, n_row)
            here = pl.ds(pl.multiple_of(other * ROW_DEV, ROW_DEV), ROW_DEV)
            mine.append(copy(
                sub_sum.at[q, :, here, :], row_in.at[q, k - 1],
                row_send.at[q, k - 1], row_recv.at[q, k - 1], {"frow": other},
            ))
        for one in mine:
            one.start()
        rows_sent.append(mine)
        started += mine
    pairs = []
    for q in range(n_chunk):
        own = pl.ds(pl.multiple_of(row * ROW_DEV, ROW_DEV), ROW_DEV)
        total = sub_sum[q, :, own, :]
        for k in range(1, n_row):
            rows_sent[q][k - 1].wait_recv()
            total = total + row_in[q, k - 1]
        row_sum[q] = total
        out_ref[col * n_chunk + q] = total
        one = copy(row_sum.at[q], pair_in.at[q], pair_send.at[q], pair_recv.at[q], {"fcol": partner})
        one.start()
        pairs.append(one)
    started += pairs
    for q in range(n_chunk):
        pairs[q].wait_recv()
        out_ref[partner * n_chunk + q] = pair_in[q]
    for one in started:
        one.wait_send()


def sum_rows(partial_sum):
    chunks, _, rows, lanes = partial_sum.shape
    n_sub, n_row = lax.axis_size("sub"), lax.axis_size("frow")
    q = chunks // 2
    f32 = jnp.float32
    dma = pltpu.SemaphoreType.DMA
    return pl.pallas_call(
        functools.partial(sum_kernel, (n_sub, n_row, q)),
        out_shape=jax.ShapeDtypeStruct((chunks, 2, ROW_DEV, lanes), f32),
        in_specs=[pl.BlockSpec(memory_space=pltpu.VMEM)],
        out_specs=pl.BlockSpec(memory_space=pltpu.VMEM),
        scratch_shapes=[
            pltpu.VMEM((q, 2, rows, lanes), f32),
            pltpu.VMEM((q, 2, rows, lanes), f32),
            pltpu.VMEM((q, n_sub - 1, 2, rows // n_sub, lanes), f32),
            pltpu.VMEM((q, 2, rows // n_sub, lanes), f32),
            pltpu.VMEM((q, n_row - 1, 2, ROW_DEV, lanes), f32),
            pltpu.VMEM((q, 2, ROW_DEV, lanes), f32),
            pltpu.VMEM((q, 2, ROW_DEV, lanes), f32),
            dma((q,)), dma((q,)),
            dma((q, n_sub - 1)), dma((q, n_sub - 1)),
            dma((q, n_row - 1)), dma((q, n_row - 1)),
            dma((q,)), dma((q,)),
        ],
        compiler_params=pltpu.CompilerParams(
            collective_id=0, has_side_effects=True, vmem_limit_bytes=VMEM_BYTES
        ),
        name="sum_rows",
    )(partial_sum)


def local(subgrids, window, counts, nonempty, column_u):
    n_blocks = lax.axis_size("sub") * lax.axis_size("frow")
    rows = ROW_DEV * n_blocks
    partial_sum = column_partial(subgrids, window, counts, nonempty, rows)
    n_local = IMAGE // FACET // lax.axis_size("fcol")
    return facet_rows(sum_rows(partial_sum), column_u, n_local)


def solution(mesh):
    return jax.shard_map(
        local,
        mesh=mesh,
        in_specs=(
            P("sub", None, ("frow", "fcol"), None),
            P(("frow", "fcol"), None),
            P("sub"),
            P("sub"),
            P(),
        ),
        out_specs=P("fcol", None, ("sub", "frow"), None),
        check_vma=False,
    )
```

```python
import functools
import math

import jax
import jax.numpy as jnp
from jax import lax
from jax.experimental import pallas as pl
from jax.experimental.pallas import tpu as pltpu
from jax.sharding import PartitionSpec as P

IMAGE = 65536
FACET = 8192
M = 512
ROW_DEV = 32
LANES = 128
VMEM_BYTES = 56 * 1024 * 1024


def sincos(k):
    q = (k + 16384) >> 15
    y = (k - (q << 15)).astype(jnp.float32) * (math.pi / IMAGE)
    z = y * y
    c = 1.0 + z * (-1.0 / 2 + z * (1.0 / 24 + z * (-1.0 / 720 + z * (1.0 / 40320))))
    s = y * (1.0 + z * (-1.0 / 6 + z * (1.0 / 120 + z * (-1.0 / 5040))))
    swap = (q & 1) == 1
    cos_part = jnp.where(swap, s, c)
    sin_part = jnp.where(swap, c, s)
    cos_part = jnp.where(((q + 1) & 2) != 0, -cos_part, cos_part)
    sin_part = jnp.where((q & 2) != 0, -sin_part, sin_part)
    return cos_part, sin_part


def split(x):
    high = x.astype(jnp.bfloat16)
    low = (x - high.astype(jnp.float32)).astype(jnp.bfloat16)
    return high, low


def reverse_rows(x):
    index = 7 - lax.broadcasted_iota(jnp.int32, (8, LANES), 0)
    n = x.shape[0] // 8
    parts = [jnp.take_along_axis(x[(n - 1 - i) * 8 : (n - i) * 8], index, axis=0) for i in range(n)]
    return jnp.concatenate(parts, 0)


def column_kernel(group, count_ref, pos_ref, sub_ref, win_ref, out_ref, left, rot, xs_even, xs_odd, acc):
    cap, _, v_count, _ = sub_ref.shape
    rows = out_ref.shape[2]
    half = rows // 2
    depth = group * v_count
    n_pairs = (count_ref[0] + 2 * group - 1) // (2 * group)
    n_groups = 2 * n_pairs
    v_start = (lax.axis_index("frow") * lax.axis_size("fcol") + lax.axis_index("fcol")) * v_count

    @pl.when(pl.program_id(0) == 0)
    def _():
        def one_slot(slot, carry):
            v = lax.broadcasted_iota(jnp.int32, (v_count, LANES), 0) + v_start
            n = v + M * jnp.maximum(pos_ref[slot], 0)
            cos_part, sin_part = sincos((rows - 1) * n)
            live = jnp.where(slot < count_ref[0], 1.0, 0.0)
            rot[slot, 0] = cos_part * live
            rot[slot, 1] = sin_part * live
            return carry

        lax.fori_loop(0, n_groups * group, one_slot, 0)
        step = 32

        def one_block(item, carry):
            g = item // (half // step)
            r = item % (half // step)
            lane = lax.broadcasted_iota(jnp.int32, (1, depth), 1)
            slot_of = lane // v_count
            p = jnp.zeros((1, depth), jnp.int32)
            for s in range(group):
                p = jnp.where(slot_of == s, jnp.maximum(pos_ref[g * group + s], 0), p)
            n = lane % v_count + v_start + M * p
            d = lax.broadcasted_iota(jnp.int32, (step, 1), 0) + r * step
            cos_part, sin_part = sincos((2 * d + 1) * n)
            for part, base in ((cos_part, 0), (sin_part, half)):
                high, low = split(part)
                here = pl.ds(pl.multiple_of(base + r * step, step), step)
                left[g, here, 0:depth] = high
                left[g, here, depth : 2 * depth] = low
                left[g, here, 2 * depth : 3 * depth] = high
            return carry

        lax.fori_loop(0, n_groups * (half // step), one_block, 0)

    acc[...] = jnp.zeros_like(acc)

    def build(g, xs):
        for s in range(group):
            slot = g * group + s
            wc = win_ref[...] * rot[slot, 0]
            ws = win_ref[...] * rot[slot, 1]
            xr, xi = sub_ref[slot, 0], sub_ref[slot, 1]
            x = jnp.concatenate([xr * wc - xi * ws, xr * ws + xi * wc], 1)
            high, low = split(x)
            xs[s * v_count : (s + 1) * v_count, :] = high
            xs[depth + s * v_count : depth + (s + 1) * v_count, :] = low

    def multiply(g, xs):
        high = xs[0:depth, :]
        right = jnp.concatenate([high, high, xs[depth : 2 * depth, :]], 0)
        acc[...] += jnp.dot(left[g], right, preferred_element_type=jnp.float32)

    build(0, xs_even)

    def one_pair(i, carry):
        build(2 * i + 1, xs_odd)
        multiply(2 * i, xs_even)
        build(jnp.minimum(2 * i + 2, n_groups - 1), xs_even)
        multiply(2 * i + 1, xs_odd)
        return carry

    lax.fori_loop(0, n_pairs, one_pair, 0)
    n_low = half // ROW_DEV
    for k in range(n_low):
        d = slice(k * ROW_DEV, (k + 1) * ROW_DEV)
        e = slice(half + k * ROW_DEV, half + (k + 1) * ROW_DEV)
        cr, ci = acc[d, :LANES], acc[d, LANES:]
        sr, si = acc[e, :LANES], acc[e, LANES:]
        out_ref[0, 0, e, :] = cr - si
        out_ref[0, 1, e, :] = sr + ci
        lower = slice((n_low - 1 - k) * ROW_DEV, (n_low - k) * ROW_DEV)
        out_ref[0, 0, lower, :] = reverse_rows(cr + si)
        out_ref[0, 1, lower, :] = reverse_rows(ci - sr)


def column_partial(subgrids, window, counts, nonempty, rows):
    cap, _, v_count, width = subgrids.shape
    group = min(8, cap // 2)
    depth = group * v_count
    flops = 2 * rows * 2 * width * cap * v_count * 3
    return pl.pallas_call(
        functools.partial(column_kernel, group),
        grid=(width // LANES,),
        out_shape=jax.ShapeDtypeStruct((width // LANES, 2, rows, LANES), jnp.float32),
        in_specs=[
            pl.BlockSpec(memory_space=pltpu.SMEM),
            pl.BlockSpec(memory_space=pltpu.SMEM),
            pl.BlockSpec((cap, 2, v_count, LANES), lambda t: (0, 0, 0, t)),
            pl.BlockSpec((v_count, LANES), lambda t: (0, t)),
        ],
        out_specs=pl.BlockSpec((1, 2, rows, LANES), lambda t: (t, 0, 0, 0)),
        scratch_shapes=[
            pltpu.VMEM((cap // group, rows, 3 * depth), jnp.bfloat16),
            pltpu.VMEM((cap, 2, v_count, LANES), jnp.float32),
            pltpu.VMEM((2 * depth, 2 * LANES), jnp.bfloat16),
            pltpu.VMEM((2 * depth, 2 * LANES), jnp.bfloat16),
            pltpu.VMEM((rows, 2 * LANES), jnp.float32),
        ],
        compiler_params=pltpu.CompilerParams(vmem_limit_bytes=VMEM_BYTES),
        cost_estimate=pl.CostEstimate(flops=flops, bytes_accessed=12 << 20, transcendentals=0),
        name="column_sum",
    )(counts, nonempty, subgrids, window)


TILE = 512


def reverse_lanes(x):
    index = (LANES - 1) - lax.broadcasted_iota(jnp.int32, (x.shape[0], LANES), 1)
    n = x.shape[1] // LANES
    parts = [
        jnp.take_along_axis(x[:, (n - 1 - i) * LANES : (n - i) * LANES], index, axis=1)
        for i in range(n)
    ]
    return jnp.concatenate(parts, 1)


def facet_kernel(n_local, column_ref, sum_ref, right, out_ref, left, buf, sem):
    t = pl.program_id(0)
    steps = pl.num_programs(0)
    column = column_ref[0]
    first = lax.axis_index("fcol") * n_local
    rows = sum_ref.shape[2]
    chunks = sum_ref.shape[0]
    mid = FACET // 2

    @pl.when(t == 0)
    def _():
        u = lax.broadcasted_iota(jnp.int32, (1, M), 1)
        w = (u + column) & (IMAGE - 1)
        for j in range(n_local):
            cos_part, sin_part = sincos((2 * FACET * (first + j) + FACET - 1) * w)
            re = jnp.concatenate([sum_ref[q, 0] for q in range(chunks)], 1)
            im = jnp.concatenate([sum_ref[q, 1] for q in range(chunks)], 1)
            for part, value in ((0, re * cos_part - im * sin_part), (1, re * sin_part + im * cos_part)):
                high, low = split(value)
                here = slice((2 * j + part) * rows, (2 * j + part + 1) * rows)
                left[here, 0:M] = high
                left[here, M : 2 * M] = low
                left[here, 2 * M : 3 * M] = high

    slot = lax.rem(t, 2)

    def copies(step, place):
        upper = pltpu.make_async_copy(
            buf.at[place, 0],
            out_ref.at[:, :, :, pl.ds(pl.multiple_of(mid + step * TILE, TILE), TILE)],
            sem.at[place, 0],
        )
        lower = pltpu.make_async_copy(
            buf.at[place, 1],
            out_ref.at[:, :, :, pl.ds(pl.multiple_of(mid - (step + 1) * TILE, TILE), TILE)],
            sem.at[place, 1],
        )
        return upper, lower

    @pl.when(t >= 2)
    def _():
        for copy in copies(t - 2, slot):
            copy.wait()

    n_tiles = TILE // LANES
    for k in range(n_tiles):
        high = right[k, 0:M, :]
        both = jnp.concatenate([high, high, right[k, M : 2 * M, :]], 0)
        products = jnp.dot(left[...], both, preferred_element_type=jnp.float32)
        upper = slice(k * LANES, (k + 1) * LANES)
        lower = slice((n_tiles - 1 - k) * LANES, (n_tiles - k) * LANES)
        for j in range(n_local):
            product = products[2 * j * rows : 2 * (j + 1) * rows]
            rc, rs = product[:rows, :LANES], product[:rows, LANES:]
            ic, is_ = product[rows:, :LANES], product[rows:, LANES:]
            buf[slot, 0, j, 0, :, upper] = rc - is_
            buf[slot, 0, j, 1, :, upper] = rs + ic
            buf[slot, 1, j, 0, :, lower] = reverse_lanes(rc + is_)
            buf[slot, 1, j, 1, :, lower] = reverse_lanes(ic - rs)
    for copy in copies(t, slot):
        copy.start()

    @pl.when(t == steps - 1)
    def _():
        for copy in copies(t - 1, 1 - slot):
            copy.wait()
        for copy in copies(t, slot):
            copy.wait()


def facet_rows(column_sum, table, column_u, n_local):
    rows = column_sum.shape[2]
    flops = 2 * (2 * n_local * rows) * (3 * M) * FACET
    return pl.pallas_call(
        functools.partial(facet_kernel, n_local),
        grid=(FACET // 2 // TILE,),
        out_shape=jax.ShapeDtypeStruct((n_local, 2, rows, FACET), jnp.float32),
        in_specs=[
            pl.BlockSpec(memory_space=pltpu.SMEM),
            pl.BlockSpec(column_sum.shape, lambda t: (0, 0, 0, 0)),
            pl.BlockSpec((TILE // LANES, 2 * M, 2 * LANES), lambda t: (t, 0, 0)),
        ],
        out_specs=pl.BlockSpec(memory_space=pl.ANY),
        scratch_shapes=[
            pltpu.VMEM((2 * n_local * rows, 3 * M), jnp.bfloat16),
            pltpu.VMEM((2, 2, n_local, 2, rows, TILE), jnp.float32),
            pltpu.SemaphoreType.DMA((2, 2)),
        ],
        compiler_params=pltpu.CompilerParams(vmem_limit_bytes=VMEM_BYTES),
        cost_estimate=pl.CostEstimate(flops=flops, bytes_accessed=25 << 20, transcendentals=0),
        name="facet_rows",
    )(column_u, column_sum, table)


def sum_kernel(sizes, column_ref, x_ref, out_ref, table_ref, base, turn, table, table_sem, half_in, half_sum, sub_in, sub_sum, row_in, row_sum, pair_in, *sems):
    n_sub, n_row, n_chunk = sizes
    sub, row, col = lax.axis_index("sub"), lax.axis_index("frow"), lax.axis_index("fcol")
    partner = 1 - col
    barrier = pltpu.get_barrier_semaphore()
    targets = [{"fcol": partner}]
    targets += [{"sub": lax.rem(sub + k, n_sub)} for k in range(1, n_sub)]
    targets += [{"frow": lax.rem(row + k, n_row)} for k in range(1, n_row)]
    for target in targets:
        pl.semaphore_signal(barrier, inc=1, device_id=target, device_id_type=pl.DeviceIdType.MESH)
    pl.semaphore_wait(barrier, len(targets))
    half_send, half_recv, sub_send, sub_recv, row_send, row_recv, pair_send, pair_recv = sems
    sub_rows = half_sum.shape[2] // n_sub

    def copy(src, dst, send, recv, target):
        return pltpu.make_async_remote_copy(
            src_ref=src, dst_ref=dst, send_sem=send, recv_sem=recv,
            device_id=target, device_id_type=pl.DeviceIdType.MESH,
        )

    started = []
    halves = [
        copy(x_ref.at[partner * n_chunk + q], half_in.at[q], half_send.at[q], half_recv.at[q], {"fcol": partner})
        for q in range(n_chunk)
    ]
    for one in halves:
        one.start()
    started += halves
    n_tiles = TILE // LANES
    n_steps = FACET // 2 // TILE

    def first_tile(i, carry):
        here = pl.ds(pl.multiple_of(i * 16, 16), 16)
        w = (lax.broadcasted_iota(jnp.int32, (16, LANES), 0) + i * 16 + column_ref[0]) & (IMAGE - 1)
        d = lax.broadcasted_iota(jnp.int32, (16, LANES), 1)
        base[0, here, :], base[1, here, :] = sincos((2 * d + 1) * w)
        turn[0, here, :], turn[1, here, :] = sincos(2 * LANES * w)
        return carry

    lax.fori_loop(0, M // 16, first_tile, 0)

    def build(step):
        def one_block(i, carry):
            here = pl.ds(pl.multiple_of(i * 16, 16), 16)
            low_here = pl.ds(pl.multiple_of(M + i * 16, 16), 16)
            c, s = base[0, here, :], base[1, here, :]
            tc, ts = turn[0, here, :], turn[1, here, :]
            for k in range(n_tiles):
                for part, value in ((0, c), (1, s)):
                    high, low = split(value)
                    place = slice(part * LANES, (part + 1) * LANES)
                    table[step * n_tiles + k, here, place] = high
                    table[step * n_tiles + k, low_here, place] = low
                c, s = c * tc - s * ts, c * ts + s * tc
            base[0, here, :], base[1, here, :] = c, s
            return carry

        lax.fori_loop(0, M // 16, one_block, 0)
        tiles = slice(step * n_tiles, (step + 1) * n_tiles)
        one = pltpu.make_async_copy(table.at[tiles], table_ref.at[tiles], table_sem.at[step])
        one.start()
        return one

    subs = []
    for q in range(n_chunk):
        halves[q].wait_recv()
        half_sum[q] = x_ref[col * n_chunk + q] + half_in[q]
        mine = []
        for k in range(1, n_sub):
            other = lax.rem(sub + k, n_sub)
            here = pl.ds(pl.multiple_of(other * sub_rows, sub_rows), sub_rows)
            mine.append(copy(
                half_sum.at[q, :, here, :], sub_in.at[q, k - 1],
                sub_send.at[q, k - 1], sub_recv.at[q, k - 1], {"sub": other},
            ))
        for one in mine:
            one.start()
        subs.append(mine)
        started += mine
    built = [build(step) for step in range(n_steps // 2)]
    rows_sent = []
    for q in range(n_chunk):
        own = pl.ds(pl.multiple_of(sub * sub_rows, sub_rows), sub_rows)
        total = half_sum[q, :, own, :]
        for k in range(1, n_sub):
            subs[q][k - 1].wait_recv()
            total = total + sub_in[q, k - 1]
        sub_sum[q] = total
        mine = []
        for k in range(1, n_row):
            other = lax.rem(row + k, n_row)
            here = pl.ds(pl.multiple_of(other * ROW_DEV, ROW_DEV), ROW_DEV)
            mine.append(copy(
                sub_sum.at[q, :, here, :], row_in.at[q, k - 1],
                row_send.at[q, k - 1], row_recv.at[q, k - 1], {"frow": other},
            ))
        for one in mine:
            one.start()
        rows_sent.append(mine)
        started += mine
        if q == 0:
            built += [build(step) for step in range(n_steps // 2, n_steps - 1)]
    built.append(build(n_steps - 1))
    pairs = []
    for q in range(n_chunk):
        own = pl.ds(pl.multiple_of(row * ROW_DEV, ROW_DEV), ROW_DEV)
        total = sub_sum[q, :, own, :]
        for k in range(1, n_row):
            rows_sent[q][k - 1].wait_recv()
            total = total + row_in[q, k - 1]
        row_sum[q] = total
        out_ref[col * n_chunk + q] = total
        one = copy(row_sum.at[q], pair_in.at[q], pair_send.at[q], pair_recv.at[q], {"fcol": partner})
        one.start()
        pairs.append(one)
    started += pairs
    for q in range(n_chunk):
        pairs[q].wait_recv()
        out_ref[partner * n_chunk + q] = pair_in[q]
    for one in started:
        one.wait_send()
    for one in built:
        one.wait()


def sum_rows(partial_sum, column_u):
    chunks, _, rows, lanes = partial_sum.shape
    n_sub, n_row = lax.axis_size("sub"), lax.axis_size("frow")
    q = chunks // 2
    f32 = jnp.float32
    dma = pltpu.SemaphoreType.DMA
    return pl.pallas_call(
        functools.partial(sum_kernel, (n_sub, n_row, q)),
        out_shape=(
            jax.ShapeDtypeStruct((chunks, 2, ROW_DEV, lanes), f32),
            jax.ShapeDtypeStruct((FACET // 2 // LANES, 2 * M, 2 * LANES), jnp.bfloat16),
        ),
        in_specs=[
            pl.BlockSpec(memory_space=pltpu.SMEM),
            pl.BlockSpec(memory_space=pltpu.VMEM),
        ],
        out_specs=(pl.BlockSpec(memory_space=pltpu.VMEM), pl.BlockSpec(memory_space=pl.ANY)),
        scratch_shapes=[
            pltpu.VMEM((2, M, LANES), f32),
            pltpu.VMEM((2, M, LANES), f32),
            pltpu.VMEM((FACET // 2 // LANES, 2 * M, 2 * LANES), jnp.bfloat16),
            dma((FACET // 2 // TILE,)),
            pltpu.VMEM((q, 2, rows, lanes), f32),
            pltpu.VMEM((q, 2, rows, lanes), f32),
            pltpu.VMEM((q, n_sub - 1, 2, rows // n_sub, lanes), f32),
            pltpu.VMEM((q, 2, rows // n_sub, lanes), f32),
            pltpu.VMEM((q, n_row - 1, 2, ROW_DEV, lanes), f32),
            pltpu.VMEM((q, 2, ROW_DEV, lanes), f32),
            pltpu.VMEM((q, 2, ROW_DEV, lanes), f32),
            dma((q,)), dma((q,)),
            dma((q, n_sub - 1)), dma((q, n_sub - 1)),
            dma((q, n_row - 1)), dma((q, n_row - 1)),
            dma((q,)), dma((q,)),
        ],
        compiler_params=pltpu.CompilerParams(
            collective_id=0, has_side_effects=True, vmem_limit_bytes=VMEM_BYTES
        ),
        name="sum_rows",
    )(column_u, partial_sum)


def local(subgrids, window, counts, nonempty, column_u):
    n_blocks = lax.axis_size("sub") * lax.axis_size("frow")
    rows = ROW_DEV * n_blocks
    partial_sum = column_partial(subgrids, window, counts, nonempty, rows)
    n_local = IMAGE // FACET // lax.axis_size("fcol")
    column_sum, table = sum_rows(partial_sum, column_u)
    return facet_rows(column_sum, table, column_u, n_local)


def solution(mesh):
    return jax.shard_map(
        local,
        mesh=mesh,
        in_specs=(
            P("sub", None, ("frow", "fcol"), None),
            P(("frow", "fcol"), None),
            P("sub"),
            P("sub"),
            P(),
        ),
        out_specs=P("fcol", None, ("sub", "frow"), None),
        check_vma=False,
    )
```

```python
import functools
import math

import jax
import jax.numpy as jnp
from jax import lax
from jax.experimental import pallas as pl
from jax.experimental.pallas import tpu as pltpu
from jax.sharding import PartitionSpec as P

IMAGE = 65536
FACET = 8192
M = 512
ROW_DEV = 32
LANES = 128
VMEM_BYTES = 56 * 1024 * 1024


def sincos(k):
    q = (k + 16384) >> 15
    y = (k - (q << 15)).astype(jnp.float32) * (math.pi / IMAGE)
    z = y * y
    c = 1.0 + z * (-1.0 / 2 + z * (1.0 / 24 + z * (-1.0 / 720 + z * (1.0 / 40320))))
    s = y * (1.0 + z * (-1.0 / 6 + z * (1.0 / 120 + z * (-1.0 / 5040))))
    swap = (q & 1) == 1
    cos_part = jnp.where(swap, s, c)
    sin_part = jnp.where(swap, c, s)
    cos_part = jnp.where(((q + 1) & 2) != 0, -cos_part, cos_part)
    sin_part = jnp.where((q & 2) != 0, -sin_part, sin_part)
    return cos_part, sin_part


def split(x):
    high = x.astype(jnp.bfloat16)
    low = (x - high.astype(jnp.float32)).astype(jnp.bfloat16)
    return high, low


def reverse_rows(x):
    index = 7 - lax.broadcasted_iota(jnp.int32, (8, LANES), 0)
    n = x.shape[0] // 8
    parts = [jnp.take_along_axis(x[(n - 1 - i) * 8 : (n - i) * 8], index, axis=0) for i in range(n)]
    return jnp.concatenate(parts, 0)


def column_kernel(group, count_ref, pos_ref, sub_ref, win_ref, out_ref, left, rot, xs_even, xs_odd, acc):
    cap, _, v_count, _ = sub_ref.shape
    rows = out_ref.shape[2]
    half = rows // 2
    depth = group * v_count
    n_pairs = (count_ref[0] + 2 * group - 1) // (2 * group)
    n_groups = 2 * n_pairs
    v_start = (lax.axis_index("frow") * lax.axis_size("fcol") + lax.axis_index("fcol")) * v_count

    @pl.when(pl.program_id(0) == 0)
    def _():
        def one_slot(slot, carry):
            v = lax.broadcasted_iota(jnp.int32, (v_count, LANES), 0) + v_start
            n = v + M * jnp.maximum(pos_ref[slot], 0)
            cos_part, sin_part = sincos((rows - 1) * n)
            live = jnp.where(slot < count_ref[0], 1.0, 0.0)
            rot[slot, 0] = cos_part * live
            rot[slot, 1] = sin_part * live
            return carry

        lax.fori_loop(0, n_groups * group, one_slot, 0)
        step = 32

        def one_block(item, carry):
            g = item // (half // step)
            r = item % (half // step)
            lane = lax.broadcasted_iota(jnp.int32, (1, depth), 1)
            slot_of = lane // v_count
            p = jnp.zeros((1, depth), jnp.int32)
            for s in range(group):
                p = jnp.where(slot_of == s, jnp.maximum(pos_ref[g * group + s], 0), p)
            n = lane % v_count + v_start + M * p
            d = lax.broadcasted_iota(jnp.int32, (step, 1), 0) + r * step
            cos_part, sin_part = sincos((2 * d + 1) * n)
            for part, base in ((cos_part, 0), (sin_part, half)):
                high, low = split(part)
                here = pl.ds(pl.multiple_of(base + r * step, step), step)
                left[g, here, 0:depth] = high
                left[g, here, depth : 2 * depth] = low
                left[g, here, 2 * depth : 3 * depth] = high
            return carry

        lax.fori_loop(0, n_groups * (half // step), one_block, 0)

    acc[...] = jnp.zeros_like(acc)

    def build(g, xs):
        for s in range(group):
            slot = g * group + s
            wc = win_ref[...] * rot[slot, 0]
            ws = win_ref[...] * rot[slot, 1]
            xr, xi = sub_ref[slot, 0], sub_ref[slot, 1]
            x = jnp.concatenate([xr * wc - xi * ws, xr * ws + xi * wc], 1)
            high, low = split(x)
            xs[s * v_count : (s + 1) * v_count, :] = high
            xs[depth + s * v_count : depth + (s + 1) * v_count, :] = low

    def multiply(g, xs):
        high = xs[0:depth, :]
        right = jnp.concatenate([high, high, xs[depth : 2 * depth, :]], 0)
        acc[...] += jnp.dot(left[g], right, preferred_element_type=jnp.float32)

    build(0, xs_even)

    def one_pair(i, carry):
        build(2 * i + 1, xs_odd)
        multiply(2 * i, xs_even)
        build(jnp.minimum(2 * i + 2, n_groups - 1), xs_even)
        multiply(2 * i + 1, xs_odd)
        return carry

    lax.fori_loop(0, n_pairs, one_pair, 0)
    n_low = half // ROW_DEV
    for k in range(n_low):
        d = slice(k * ROW_DEV, (k + 1) * ROW_DEV)
        e = slice(half + k * ROW_DEV, half + (k + 1) * ROW_DEV)
        cr, ci = acc[d, :LANES], acc[d, LANES:]
        sr, si = acc[e, :LANES], acc[e, LANES:]
        out_ref[0, 0, e, :] = cr - si
        out_ref[0, 1, e, :] = sr + ci
        lower = slice((n_low - 1 - k) * ROW_DEV, (n_low - k) * ROW_DEV)
        out_ref[0, 0, lower, :] = reverse_rows(cr + si)
        out_ref[0, 1, lower, :] = reverse_rows(ci - sr)


def column_partial(subgrids, window, counts, nonempty, rows):
    cap, _, v_count, width = subgrids.shape
    group = min(8, cap // 2)
    depth = group * v_count
    flops = 2 * rows * 2 * width * cap * v_count * 3
    return pl.pallas_call(
        functools.partial(column_kernel, group),
        grid=(width // LANES,),
        out_shape=jax.ShapeDtypeStruct((width // LANES, 2, rows, LANES), jnp.float32),
        in_specs=[
            pl.BlockSpec(memory_space=pltpu.SMEM),
            pl.BlockSpec(memory_space=pltpu.SMEM),
            pl.BlockSpec((cap, 2, v_count, LANES), lambda t: (0, 0, 0, t)),
            pl.BlockSpec((v_count, LANES), lambda t: (0, t)),
        ],
        out_specs=pl.BlockSpec((1, 2, rows, LANES), lambda t: (t, 0, 0, 0)),
        scratch_shapes=[
            pltpu.VMEM((cap // group, rows, 3 * depth), jnp.bfloat16),
            pltpu.VMEM((cap, 2, v_count, LANES), jnp.float32),
            pltpu.VMEM((2 * depth, 2 * LANES), jnp.bfloat16),
            pltpu.VMEM((2 * depth, 2 * LANES), jnp.bfloat16),
            pltpu.VMEM((rows, 2 * LANES), jnp.float32),
        ],
        compiler_params=pltpu.CompilerParams(vmem_limit_bytes=VMEM_BYTES),
        cost_estimate=pl.CostEstimate(flops=flops, bytes_accessed=12 << 20, transcendentals=0),
        name="column_sum",
    )(counts, nonempty, subgrids, window)


TILE = 512


def reverse_lanes(x):
    index = (LANES - 1) - lax.broadcasted_iota(jnp.int32, (x.shape[0], LANES), 1)
    n = x.shape[1] // LANES
    parts = [
        jnp.take_along_axis(x[:, (n - 1 - i) * LANES : (n - i) * LANES], index, axis=1)
        for i in range(n)
    ]
    return jnp.concatenate(parts, 1)


def facet_kernel(n_local, column_ref, sum_ref, right, out_ref, left, buf, sem):
    t = pl.program_id(0)
    steps = pl.num_programs(0)
    column = column_ref[0]
    first = lax.axis_index("fcol") * n_local
    rows = sum_ref.shape[2]
    chunks = sum_ref.shape[0]
    mid = FACET // 2
    n_left = 2 * n_local * rows

    @pl.when(t == 0)
    def _():
        u = lax.broadcasted_iota(jnp.int32, (1, M), 1)
        w = (u + column) & (IMAGE - 1)
        for j in range(n_local):
            cos_part, sin_part = sincos((2 * FACET * (first + j) + FACET - 1) * w)
            re = jnp.concatenate([sum_ref[q, 0] for q in range(chunks)], 1)
            im = jnp.concatenate([sum_ref[q, 1] for q in range(chunks)], 1)
            for part, value in ((0, re * cos_part - im * sin_part), (1, re * sin_part + im * cos_part)):
                high, low = split(value)
                here = slice((2 * j + part) * rows, (2 * j + part + 1) * rows)
                left[here, :] = high
                left[slice(here.start + n_left, here.stop + n_left), :] = low

    slot = lax.rem(t, 2)

    def copies(step, place):
        upper = pltpu.make_async_copy(
            buf.at[place, 0],
            out_ref.at[:, :, :, pl.ds(pl.multiple_of(mid + step * TILE, TILE), TILE)],
            sem.at[place, 0],
        )
        lower = pltpu.make_async_copy(
            buf.at[place, 1],
            out_ref.at[:, :, :, pl.ds(pl.multiple_of(mid - (step + 1) * TILE, TILE), TILE)],
            sem.at[place, 1],
        )
        return upper, lower

    @pl.when(t >= 2)
    def _():
        for copy in copies(t - 2, slot):
            copy.wait()

    n_tiles = TILE // LANES
    for k in range(n_tiles):
        high = right[k, 0:M, :]
        low = right[k, M : 2 * M, :]
        stacked = jnp.dot(left[...], high, preferred_element_type=jnp.float32)
        products = jnp.dot(left[0:n_left, :], low, preferred_element_type=jnp.float32)
        products = products + stacked[:n_left] + stacked[n_left:]
        upper = slice(k * LANES, (k + 1) * LANES)
        lower = slice((n_tiles - 1 - k) * LANES, (n_tiles - k) * LANES)
        for j in range(n_local):
            product = products[2 * j * rows : 2 * (j + 1) * rows]
            rc, rs = product[:rows, :LANES], product[:rows, LANES:]
            ic, is_ = product[rows:, :LANES], product[rows:, LANES:]
            buf[slot, 0, j, 0, :, upper] = rc - is_
            buf[slot, 0, j, 1, :, upper] = rs + ic
            buf[slot, 1, j, 0, :, lower] = reverse_lanes(rc + is_)
            buf[slot, 1, j, 1, :, lower] = reverse_lanes(ic - rs)
    for copy in copies(t, slot):
        copy.start()

    @pl.when(t == steps - 1)
    def _():
        for copy in copies(t - 1, 1 - slot):
            copy.wait()
        for copy in copies(t, slot):
            copy.wait()


def facet_rows(column_sum, table, column_u, n_local):
    rows = column_sum.shape[2]
    flops = 2 * (2 * n_local * rows) * (3 * M) * FACET
    return pl.pallas_call(
        functools.partial(facet_kernel, n_local),
        grid=(FACET // 2 // TILE,),
        out_shape=jax.ShapeDtypeStruct((n_local, 2, rows, FACET), jnp.float32),
        in_specs=[
            pl.BlockSpec(memory_space=pltpu.SMEM),
            pl.BlockSpec(column_sum.shape, lambda t: (0, 0, 0, 0)),
            pl.BlockSpec((TILE // LANES, 2 * M, 2 * LANES), lambda t: (t, 0, 0)),
        ],
        out_specs=pl.BlockSpec(memory_space=pl.ANY),
        scratch_shapes=[
            pltpu.VMEM((4 * n_local * rows, M), jnp.bfloat16),
            pltpu.VMEM((2, 2, n_local, 2, rows, TILE), jnp.float32),
            pltpu.SemaphoreType.DMA((2, 2)),
        ],
        compiler_params=pltpu.CompilerParams(vmem_limit_bytes=VMEM_BYTES),
        cost_estimate=pl.CostEstimate(flops=flops, bytes_accessed=25 << 20, transcendentals=0),
        name="facet_rows",
    )(column_u, column_sum, table)


def sum_kernel(sizes, column_ref, x_ref, out_ref, table_ref, base, turn, table, table_sem, half_in, half_sum, sub_in, sub_sum, row_in, row_sum, pair_in, *sems):
    n_sub, n_row, n_chunk = sizes
    sub, row, col = lax.axis_index("sub"), lax.axis_index("frow"), lax.axis_index("fcol")
    partner = 1 - col
    barrier = pltpu.get_barrier_semaphore()
    targets = [{"fcol": partner}]
    targets += [{"sub": lax.rem(sub + k, n_sub)} for k in range(1, n_sub)]
    targets += [{"frow": lax.rem(row + k, n_row)} for k in range(1, n_row)]
    for target in targets:
        pl.semaphore_signal(barrier, inc=1, device_id=target, device_id_type=pl.DeviceIdType.MESH)
    pl.semaphore_wait(barrier, len(targets))
    half_send, half_recv, sub_send, sub_recv, row_send, row_recv, pair_send, pair_recv = sems
    sub_rows = half_sum.shape[2] // n_sub

    def copy(src, dst, send, recv, target):
        return pltpu.make_async_remote_copy(
            src_ref=src, dst_ref=dst, send_sem=send, recv_sem=recv,
            device_id=target, device_id_type=pl.DeviceIdType.MESH,
        )

    started = []
    halves = [
        copy(x_ref.at[partner * n_chunk + q], half_in.at[q], half_send.at[q], half_recv.at[q], {"fcol": partner})
        for q in range(n_chunk)
    ]
    for one in halves:
        one.start()
    started += halves
    n_tiles = TILE // LANES
    n_steps = FACET // 2 // TILE

    def first_tile(i, carry):
        here = pl.ds(pl.multiple_of(i * 16, 16), 16)
        w = (lax.broadcasted_iota(jnp.int32, (16, LANES), 0) + i * 16 + column_ref[0]) & (IMAGE - 1)
        d = lax.broadcasted_iota(jnp.int32, (16, LANES), 1)
        base[0, here, :], base[1, here, :] = sincos((2 * d + 1) * w)
        turn[0, here, :], turn[1, here, :] = sincos(2 * LANES * w)
        return carry

    lax.fori_loop(0, M // 16, first_tile, 0)

    def build(step):
        def one_block(i, carry):
            here = pl.ds(pl.multiple_of(i * 16, 16), 16)
            low_here = pl.ds(pl.multiple_of(M + i * 16, 16), 16)
            c, s = base[0, here, :], base[1, here, :]
            tc, ts = turn[0, here, :], turn[1, here, :]
            for k in range(n_tiles):
                for part, value in ((0, c), (1, s)):
                    high, low = split(value)
                    place = slice(part * LANES, (part + 1) * LANES)
                    table[step * n_tiles + k, here, place] = high
                    table[step * n_tiles + k, low_here, place] = low
                c, s = c * tc - s * ts, c * ts + s * tc
            base[0, here, :], base[1, here, :] = c, s
            return carry

        lax.fori_loop(0, M // 16, one_block, 0)
        tiles = slice(step * n_tiles, (step + 1) * n_tiles)
        one = pltpu.make_async_copy(table.at[tiles], table_ref.at[tiles], table_sem.at[step])
        one.start()
        return one

    subs = []
    for q in range(n_chunk):
        halves[q].wait_recv()
        half_sum[q] = x_ref[col * n_chunk + q] + half_in[q]
        mine = []
        for k in range(1, n_sub):
            other = lax.rem(sub + k, n_sub)
            here = pl.ds(pl.multiple_of(other * sub_rows, sub_rows), sub_rows)
            mine.append(copy(
                half_sum.at[q, :, here, :], sub_in.at[q, k - 1],
                sub_send.at[q, k - 1], sub_recv.at[q, k - 1], {"sub": other},
            ))
        for one in mine:
            one.start()
        subs.append(mine)
        started += mine
    built = [build(step) for step in range(3)]
    rows_sent = []
    for q in range(n_chunk):
        own = pl.ds(pl.multiple_of(sub * sub_rows, sub_rows), sub_rows)
        total = half_sum[q, :, own, :]
        for k in range(1, n_sub):
            subs[q][k - 1].wait_recv()
            total = total + sub_in[q, k - 1]
        sub_sum[q] = total
        mine = []
        for k in range(1, n_row):
            other = lax.rem(row + k, n_row)
            here = pl.ds(pl.multiple_of(other * ROW_DEV, ROW_DEV), ROW_DEV)
            mine.append(copy(
                sub_sum.at[q, :, here, :], row_in.at[q, k - 1],
                row_send.at[q, k - 1], row_recv.at[q, k - 1], {"frow": other},
            ))
        for one in mine:
            one.start()
        rows_sent.append(mine)
        started += mine
        if q < n_chunk - 1:
            built.append(build(3 + q))
    built += [build(step) for step in range(2 + n_chunk, n_steps)]
    pairs = []
    for q in range(n_chunk):
        own = pl.ds(pl.multiple_of(row * ROW_DEV, ROW_DEV), ROW_DEV)
        total = sub_sum[q, :, own, :]
        for k in range(1, n_row):
            rows_sent[q][k - 1].wait_recv()
            total = total + row_in[q, k - 1]
        row_sum[q] = total
        out_ref[col * n_chunk + q] = total
        one = copy(row_sum.at[q], pair_in.at[q], pair_send.at[q], pair_recv.at[q], {"fcol": partner})
        one.start()
        pairs.append(one)
    started += pairs
    for q in range(n_chunk):
        pairs[q].wait_recv()
        out_ref[partner * n_chunk + q] = pair_in[q]
    for one in started:
        one.wait_send()
    for one in built:
        one.wait()


def sum_rows(partial_sum, column_u):
    rows, lanes = partial_sum.shape[2:]
    partial_sum = partial_sum.reshape(-1, 1, rows, lanes)
    chunks = partial_sum.shape[0]
    n_sub, n_row = lax.axis_size("sub"), lax.axis_size("frow")
    q = chunks // 2
    f32 = jnp.float32
    dma = pltpu.SemaphoreType.DMA
    return pl.pallas_call(
        functools.partial(sum_kernel, (n_sub, n_row, q)),
        out_shape=(
            jax.ShapeDtypeStruct((chunks, 1, ROW_DEV, lanes), f32),
            jax.ShapeDtypeStruct((FACET // 2 // LANES, 2 * M, 2 * LANES), jnp.bfloat16),
        ),
        in_specs=[
            pl.BlockSpec(memory_space=pltpu.SMEM),
            pl.BlockSpec(memory_space=pltpu.VMEM),
        ],
        out_specs=(pl.BlockSpec(memory_space=pltpu.VMEM), pl.BlockSpec(memory_space=pl.ANY)),
        scratch_shapes=[
            pltpu.VMEM((2, M, LANES), f32),
            pltpu.VMEM((2, M, LANES), f32),
            pltpu.VMEM((FACET // 2 // LANES, 2 * M, 2 * LANES), jnp.bfloat16),
            dma((FACET // 2 // TILE,)),
            pltpu.VMEM((q, 1, rows, lanes), f32),
            pltpu.VMEM((q, 1, rows, lanes), f32),
            pltpu.VMEM((q, n_sub - 1, 1, rows // n_sub, lanes), f32),
            pltpu.VMEM((q, 1, rows // n_sub, lanes), f32),
            pltpu.VMEM((q, n_row - 1, 1, ROW_DEV, lanes), f32),
            pltpu.VMEM((q, 1, ROW_DEV, lanes), f32),
            pltpu.VMEM((q, 1, ROW_DEV, lanes), f32),
            dma((q,)), dma((q,)),
            dma((q, n_sub - 1)), dma((q, n_sub - 1)),
            dma((q, n_row - 1)), dma((q, n_row - 1)),
            dma((q,)), dma((q,)),
        ],
        compiler_params=pltpu.CompilerParams(
            collective_id=0, has_side_effects=True, vmem_limit_bytes=VMEM_BYTES
        ),
        name="sum_rows",
    )(column_u, partial_sum)


def local(subgrids, window, counts, nonempty, column_u):
    n_blocks = lax.axis_size("sub") * lax.axis_size("frow")
    rows = ROW_DEV * n_blocks
    partial_sum = column_partial(subgrids, window, counts, nonempty, rows)
    n_local = IMAGE // FACET // lax.axis_size("fcol")
    column_sum, table = sum_rows(partial_sum, column_u)
    column_sum = column_sum.reshape(-1, 2, ROW_DEV, LANES)
    return facet_rows(column_sum, table, column_u, n_local)


def solution(mesh):
    return jax.shard_map(
        local,
        mesh=mesh,
        in_specs=(
            P("sub", None, ("frow", "fcol"), None),
            P(("frow", "fcol"), None),
            P("sub"),
            P("sub"),
            P(),
        ),
        out_specs=P("fcol", None, ("sub", "frow"), None),
        check_vma=False,
    )
```

```python
import functools
import math

import jax
import jax.numpy as jnp
from jax import lax
from jax.experimental import pallas as pl
from jax.experimental.pallas import tpu as pltpu
from jax.sharding import PartitionSpec as P

IMAGE = 65536
FACET = 8192
M = 512
ROW_DEV = 32
LANES = 128
VMEM_BYTES = 56 * 1024 * 1024


def sincos(k):
    q = (k + 16384) >> 15
    y = (k - (q << 15)).astype(jnp.float32) * (math.pi / IMAGE)
    z = y * y
    c = 1.0 + z * (-1.0 / 2 + z * (1.0 / 24 + z * (-1.0 / 720 + z * (1.0 / 40320))))
    s = y * (1.0 + z * (-1.0 / 6 + z * (1.0 / 120 + z * (-1.0 / 5040))))
    swap = (q & 1) == 1
    cos_part = jnp.where(swap, s, c)
    sin_part = jnp.where(swap, c, s)
    cos_part = jnp.where(((q + 1) & 2) != 0, -cos_part, cos_part)
    sin_part = jnp.where((q & 2) != 0, -sin_part, sin_part)
    return cos_part, sin_part


def split(x):
    high = x.astype(jnp.bfloat16)
    low = (x - high.astype(jnp.float32)).astype(jnp.bfloat16)
    return high, low


def reverse_rows(x):
    index = 7 - lax.broadcasted_iota(jnp.int32, (8, LANES), 0)
    n = x.shape[0] // 8
    parts = [jnp.take_along_axis(x[(n - 1 - i) * 8 : (n - i) * 8], index, axis=0) for i in range(n)]
    return jnp.concatenate(parts, 0)


def column_kernel(group, count_ref, pos_ref, sub_ref, win_ref, out_ref, left, rot, xs_even, xs_odd, acc):
    cap, _, v_count, _ = sub_ref.shape
    rows = out_ref.shape[2]
    half = rows // 2
    depth = group * v_count
    n_pairs = (count_ref[0] + 2 * group - 1) // (2 * group)
    n_groups = 2 * n_pairs
    v_start = (lax.axis_index("frow") * lax.axis_size("fcol") + lax.axis_index("fcol")) * v_count

    @pl.when(pl.program_id(0) == 0)
    def _():
        def one_slot(slot, carry):
            v = lax.broadcasted_iota(jnp.int32, (v_count, LANES), 0) + v_start
            n = v + M * jnp.maximum(pos_ref[slot], 0)
            cos_part, sin_part = sincos((rows - 1) * n)
            live = jnp.where(slot < count_ref[0], 1.0, 0.0)
            rot[slot, 0] = cos_part * live
            rot[slot, 1] = sin_part * live
            return carry

        lax.fori_loop(0, n_groups * group, one_slot, 0)
        step = 32

        def one_block(item, carry):
            g = item // (half // step)
            r = item % (half // step)
            lane = lax.broadcasted_iota(jnp.int32, (1, depth), 1)
            slot_of = lane // v_count
            p = jnp.zeros((1, depth), jnp.int32)
            for s in range(group):
                p = jnp.where(slot_of == s, jnp.maximum(pos_ref[g * group + s], 0), p)
            n = lane % v_count + v_start + M * p
            d = lax.broadcasted_iota(jnp.int32, (step, 1), 0) + r * step
            cos_part, sin_part = sincos((2 * d + 1) * n)
            for part, base in ((cos_part, 0), (sin_part, half)):
                high, low = split(part)
                here = pl.ds(pl.multiple_of(base + r * step, step), step)
                left[g, here, 0:depth] = high
                left[g, here, depth : 2 * depth] = low
                left[g, here, 2 * depth : 3 * depth] = high
            return carry

        lax.fori_loop(0, n_groups * (half // step), one_block, 0)

    acc[...] = jnp.zeros_like(acc)

    def build(g, xs):
        for s in range(group):
            slot = g * group + s
            wc = win_ref[...] * rot[slot, 0]
            ws = win_ref[...] * rot[slot, 1]
            xr, xi = sub_ref[slot, 0], sub_ref[slot, 1]
            x = jnp.concatenate([xr * wc - xi * ws, xr * ws + xi * wc], 1)
            high, low = split(x)
            xs[s * v_count : (s + 1) * v_count, :] = high
            xs[depth + s * v_count : depth + (s + 1) * v_count, :] = low

    def multiply(g, xs):
        high = xs[0:depth, :]
        right = jnp.concatenate([high, high, xs[depth : 2 * depth, :]], 0)
        acc[...] += jnp.dot(left[g], right, preferred_element_type=jnp.float32)

    build(0, xs_even)

    def one_pair(i, carry):
        build(2 * i + 1, xs_odd)
        multiply(2 * i, xs_even)
        build(jnp.minimum(2 * i + 2, n_groups - 1), xs_even)
        multiply(2 * i + 1, xs_odd)
        return carry

    lax.fori_loop(0, n_pairs, one_pair, 0)
    n_low = half // ROW_DEV
    for k in range(n_low):
        d = slice(k * ROW_DEV, (k + 1) * ROW_DEV)
        e = slice(half + k * ROW_DEV, half + (k + 1) * ROW_DEV)
        cr, ci = acc[d, :LANES], acc[d, LANES:]
        sr, si = acc[e, :LANES], acc[e, LANES:]
        out_ref[0, 0, e, :] = cr - si
        out_ref[0, 1, e, :] = sr + ci
        lower = slice((n_low - 1 - k) * ROW_DEV, (n_low - k) * ROW_DEV)
        out_ref[0, 0, lower, :] = reverse_rows(cr + si)
        out_ref[0, 1, lower, :] = reverse_rows(ci - sr)


def column_partial(subgrids, window, counts, nonempty, rows):
    cap, _, v_count, width = subgrids.shape
    group = min(8, cap // 2)
    depth = group * v_count
    flops = 2 * rows * 2 * width * cap * v_count * 3
    return pl.pallas_call(
        functools.partial(column_kernel, group),
        grid=(width // LANES,),
        out_shape=jax.ShapeDtypeStruct((width // LANES, 2, rows, LANES), jnp.float32),
        in_specs=[
            pl.BlockSpec(memory_space=pltpu.SMEM),
            pl.BlockSpec(memory_space=pltpu.SMEM),
            pl.BlockSpec((cap, 2, v_count, LANES), lambda t: (0, 0, 0, t)),
            pl.BlockSpec((v_count, LANES), lambda t: (0, t)),
        ],
        out_specs=pl.BlockSpec((1, 2, rows, LANES), lambda t: (t, 0, 0, 0)),
        scratch_shapes=[
            pltpu.VMEM((cap // group, rows, 3 * depth), jnp.bfloat16),
            pltpu.VMEM((cap, 2, v_count, LANES), jnp.float32),
            pltpu.VMEM((2 * depth, 2 * LANES), jnp.bfloat16),
            pltpu.VMEM((2 * depth, 2 * LANES), jnp.bfloat16),
            pltpu.VMEM((rows, 2 * LANES), jnp.float32),
        ],
        compiler_params=pltpu.CompilerParams(vmem_limit_bytes=VMEM_BYTES),
        cost_estimate=pl.CostEstimate(flops=flops, bytes_accessed=12 << 20, transcendentals=0),
        name="column_sum",
    )(counts, nonempty, subgrids, window)


TILE = 512


def reverse_lanes(x):
    index = (LANES - 1) - lax.broadcasted_iota(jnp.int32, (x.shape[0], LANES), 1)
    n = x.shape[1] // LANES
    parts = [
        jnp.take_along_axis(x[:, (n - 1 - i) * LANES : (n - i) * LANES], index, axis=1)
        for i in range(n)
    ]
    return jnp.concatenate(parts, 1)


def facet_kernel(n_local, column_ref, sum_ref, right, out_ref, left, buf, sem):
    t = pl.program_id(0)
    steps = pl.num_programs(0)
    column = column_ref[0]
    first = lax.axis_index("fcol") * n_local
    rows = sum_ref.shape[2]
    chunks = sum_ref.shape[0]
    mid = FACET // 2
    n_left = 2 * n_local * rows

    @pl.when(t == 0)
    def _():
        u = lax.broadcasted_iota(jnp.int32, (1, M), 1)
        w = (u + column) & (IMAGE - 1)
        for j in range(n_local):
            cos_part, sin_part = sincos((2 * FACET * (first + j) + FACET - 1) * w)
            re = jnp.concatenate([sum_ref[q, 0] for q in range(chunks)], 1)
            im = jnp.concatenate([sum_ref[q, 1] for q in range(chunks)], 1)
            for part, value in ((0, re * cos_part - im * sin_part), (1, re * sin_part + im * cos_part)):
                high, low = split(value)
                here = slice((2 * j + part) * rows, (2 * j + part + 1) * rows)
                left[here, :] = high
                left[slice(here.start + n_left, here.stop + n_left), :] = low

    slot = lax.rem(t, 2)

    def copies(step, place):
        upper = pltpu.make_async_copy(
            buf.at[place, 0],
            out_ref.at[:, :, :, pl.ds(pl.multiple_of(mid + step * TILE, TILE), TILE)],
            sem.at[place, 0],
        )
        lower = pltpu.make_async_copy(
            buf.at[place, 1],
            out_ref.at[:, :, :, pl.ds(pl.multiple_of(mid - (step + 1) * TILE, TILE), TILE)],
            sem.at[place, 1],
        )
        return upper, lower

    @pl.when(t >= 2)
    def _():
        for copy in copies(t - 2, slot):
            copy.wait()

    n_tiles = TILE // LANES
    for k in range(n_tiles):
        high = right[k, 0:M, :]
        low = right[k, M : 2 * M, :]
        stacked = jnp.dot(left[...], high, preferred_element_type=jnp.float32)
        products = jnp.dot(left[0:n_left, :], low, preferred_element_type=jnp.float32)
        products = products + stacked[:n_left] + stacked[n_left:]
        upper = slice(k * LANES, (k + 1) * LANES)
        lower = slice((n_tiles - 1 - k) * LANES, (n_tiles - k) * LANES)
        for j in range(n_local):
            product = products[2 * j * rows : 2 * (j + 1) * rows]
            rc, rs = product[:rows, :LANES], product[:rows, LANES:]
            ic, is_ = product[rows:, :LANES], product[rows:, LANES:]
            buf[slot, 0, j, 0, :, upper] = rc - is_
            buf[slot, 0, j, 1, :, upper] = rs + ic
            buf[slot, 1, j, 0, :, lower] = reverse_lanes(rc + is_)
            buf[slot, 1, j, 1, :, lower] = reverse_lanes(ic - rs)
    for copy in copies(t, slot):
        copy.start()

    @pl.when(t == steps - 1)
    def _():
        for copy in copies(t - 1, 1 - slot):
            copy.wait()
        for copy in copies(t, slot):
            copy.wait()


def facet_rows(column_sum, table, column_u, n_local):
    rows = column_sum.shape[2]
    flops = 2 * (2 * n_local * rows) * (3 * M) * FACET
    return pl.pallas_call(
        functools.partial(facet_kernel, n_local),
        grid=(FACET // 2 // TILE,),
        out_shape=jax.ShapeDtypeStruct((n_local, 2, rows, FACET), jnp.float32),
        in_specs=[
            pl.BlockSpec(memory_space=pltpu.SMEM),
            pl.BlockSpec(column_sum.shape, lambda t: (0, 0, 0, 0)),
            pl.BlockSpec((TILE // LANES, 2 * M, 2 * LANES), lambda t: (t, 0, 0)),
        ],
        out_specs=pl.BlockSpec(memory_space=pl.ANY),
        scratch_shapes=[
            pltpu.VMEM((4 * n_local * rows, M), jnp.bfloat16),
            pltpu.VMEM((2, 2, n_local, 2, rows, TILE), jnp.float32),
            pltpu.SemaphoreType.DMA((2, 2)),
        ],
        compiler_params=pltpu.CompilerParams(vmem_limit_bytes=VMEM_BYTES),
        cost_estimate=pl.CostEstimate(flops=flops, bytes_accessed=25 << 20, transcendentals=0),
        name="facet_rows",
    )(column_u, column_sum, table)


def sum_kernel(sizes, column_ref, x_ref, out_ref, table_ref, base, turn, table, table_sem, half_in, half_sum, sub_in, sub_sum, row_in, row_sum, pair_in, *sems):
    n_sub, n_row, n_chunk = sizes
    sub, row, col = lax.axis_index("sub"), lax.axis_index("frow"), lax.axis_index("fcol")
    partner = 1 - col
    barrier = pltpu.get_barrier_semaphore()
    targets = [{"fcol": partner}]
    targets += [{"sub": lax.rem(sub + k, n_sub)} for k in range(1, n_sub)]
    targets += [{"frow": lax.rem(row + k, n_row)} for k in range(1, n_row)]
    for target in targets:
        pl.semaphore_signal(barrier, inc=1, device_id=target, device_id_type=pl.DeviceIdType.MESH)
    pl.semaphore_wait(barrier, len(targets))
    half_send, half_recv, sub_send, sub_recv, row_send, row_recv, pair_send, pair_recv = sems
    sub_rows = half_sum.shape[2] // n_sub

    def copy(src, dst, send, recv, target):
        return pltpu.make_async_remote_copy(
            src_ref=src, dst_ref=dst, send_sem=send, recv_sem=recv,
            device_id=target, device_id_type=pl.DeviceIdType.MESH,
        )

    started = []
    halves = [
        copy(x_ref.at[partner * n_chunk + q], half_in.at[q], half_send.at[q], half_recv.at[q], {"fcol": partner})
        for q in range(n_chunk)
    ]
    for one in halves:
        one.start()
    started += halves
    n_tiles = TILE // LANES
    n_steps = FACET // 2 // TILE

    def first_tile(i, carry):
        here = pl.ds(pl.multiple_of(i * 16, 16), 16)
        w = (lax.broadcasted_iota(jnp.int32, (16, LANES), 0) + i * 16 + column_ref[0]) & (IMAGE - 1)
        d = lax.broadcasted_iota(jnp.int32, (16, LANES), 1)
        base[0, here, :], base[1, here, :] = sincos((2 * d + 1) * w)
        turn[0, here, :], turn[1, here, :] = sincos(2 * LANES * w)
        return carry

    lax.fori_loop(0, M // 16, first_tile, 0, unroll=2)

    def build(step):
        def one_block(i, carry):
            here = pl.ds(pl.multiple_of(i * 16, 16), 16)
            low_here = pl.ds(pl.multiple_of(M + i * 16, 16), 16)
            c, s = base[0, here, :], base[1, here, :]
            tc, ts = turn[0, here, :], turn[1, here, :]
            for k in range(n_tiles):
                for part, value in ((0, c), (1, s)):
                    high, low = split(value)
                    place = slice(part * LANES, (part + 1) * LANES)
                    table[step * n_tiles + k, here, place] = high
                    table[step * n_tiles + k, low_here, place] = low
                c, s = c * tc - s * ts, c * ts + s * tc
            base[0, here, :], base[1, here, :] = c, s
            return carry

        lax.fori_loop(0, M // 16, one_block, 0, unroll=2)
        tiles = slice(step * n_tiles, (step + 1) * n_tiles)
        one = pltpu.make_async_copy(table.at[tiles], table_ref.at[tiles], table_sem.at[step])
        one.start()
        return one

    subs = []
    for q in range(n_chunk):
        halves[q].wait_recv()
        half_sum[q] = x_ref[col * n_chunk + q] + half_in[q]
        mine = []
        for k in range(1, n_sub):
            other = lax.rem(sub + k, n_sub)
            here = pl.ds(pl.multiple_of(other * sub_rows, sub_rows), sub_rows)
            mine.append(copy(
                half_sum.at[q, :, here, :], sub_in.at[q, k - 1],
                sub_send.at[q, k - 1], sub_recv.at[q, k - 1], {"sub": other},
            ))
        for one in mine:
            one.start()
        subs.append(mine)
        started += mine
    built = [build(step) for step in range(3)]
    rows_sent = []
    for q in range(n_chunk):
        own = pl.ds(pl.multiple_of(sub * sub_rows, sub_rows), sub_rows)
        total = half_sum[q, :, own, :]
        for k in range(1, n_sub):
            subs[q][k - 1].wait_recv()
            total = total + sub_in[q, k - 1]
        sub_sum[q] = total
        mine = []
        for k in range(1, n_row):
            other = lax.rem(row + k, n_row)
            here = pl.ds(pl.multiple_of(other * ROW_DEV, ROW_DEV), ROW_DEV)
            mine.append(copy(
                sub_sum.at[q, :, here, :], row_in.at[q, k - 1],
                row_send.at[q, k - 1], row_recv.at[q, k - 1], {"frow": other},
            ))
        for one in mine:
            one.start()
        rows_sent.append(mine)
        started += mine
        if q < n_chunk - 1:
            built.append(build(3 + q))
    built += [build(step) for step in range(2 + n_chunk, n_steps)]
    pairs = []
    for q in range(n_chunk):
        own = pl.ds(pl.multiple_of(row * ROW_DEV, ROW_DEV), ROW_DEV)
        total = sub_sum[q, :, own, :]
        for k in range(1, n_row):
            rows_sent[q][k - 1].wait_recv()
            total = total + row_in[q, k - 1]
        row_sum[q] = total
        out_ref[col * n_chunk + q] = total
        one = copy(row_sum.at[q], pair_in.at[q], pair_send.at[q], pair_recv.at[q], {"fcol": partner})
        one.start()
        pairs.append(one)
    started += pairs
    for q in range(n_chunk):
        pairs[q].wait_recv()
        out_ref[partner * n_chunk + q] = pair_in[q]
    for one in started:
        one.wait_send()
    for one in built:
        one.wait()


def sum_rows(partial_sum, column_u):
    rows, lanes = partial_sum.shape[2:]
    partial_sum = partial_sum.reshape(-1, 1, rows, lanes)
    chunks = partial_sum.shape[0]
    n_sub, n_row = lax.axis_size("sub"), lax.axis_size("frow")
    q = chunks // 2
    f32 = jnp.float32
    dma = pltpu.SemaphoreType.DMA
    return pl.pallas_call(
        functools.partial(sum_kernel, (n_sub, n_row, q)),
        out_shape=(
            jax.ShapeDtypeStruct((chunks, 1, ROW_DEV, lanes), f32),
            jax.ShapeDtypeStruct((FACET // 2 // LANES, 2 * M, 2 * LANES), jnp.bfloat16),
        ),
        in_specs=[
            pl.BlockSpec(memory_space=pltpu.SMEM),
            pl.BlockSpec(memory_space=pltpu.VMEM),
        ],
        out_specs=(pl.BlockSpec(memory_space=pltpu.VMEM), pl.BlockSpec(memory_space=pl.ANY)),
        scratch_shapes=[
            pltpu.VMEM((2, M, LANES), f32),
            pltpu.VMEM((2, M, LANES), f32),
            pltpu.VMEM((FACET // 2 // LANES, 2 * M, 2 * LANES), jnp.bfloat16),
            dma((FACET // 2 // TILE,)),
            pltpu.VMEM((q, 1, rows, lanes), f32),
            pltpu.VMEM((q, 1, rows, lanes), f32),
            pltpu.VMEM((q, n_sub - 1, 1, rows // n_sub, lanes), f32),
            pltpu.VMEM((q, 1, rows // n_sub, lanes), f32),
            pltpu.VMEM((q, n_row - 1, 1, ROW_DEV, lanes), f32),
            pltpu.VMEM((q, 1, ROW_DEV, lanes), f32),
            pltpu.VMEM((q, 1, ROW_DEV, lanes), f32),
            dma((q,)), dma((q,)),
            dma((q, n_sub - 1)), dma((q, n_sub - 1)),
            dma((q, n_row - 1)), dma((q, n_row - 1)),
            dma((q,)), dma((q,)),
        ],
        compiler_params=pltpu.CompilerParams(
            collective_id=0, has_side_effects=True, vmem_limit_bytes=VMEM_BYTES
        ),
        name="sum_rows",
    )(column_u, partial_sum)


def local(subgrids, window, counts, nonempty, column_u):
    n_blocks = lax.axis_size("sub") * lax.axis_size("frow")
    rows = ROW_DEV * n_blocks
    partial_sum = column_partial(subgrids, window, counts, nonempty, rows)
    n_local = IMAGE // FACET // lax.axis_size("fcol")
    column_sum, table = sum_rows(partial_sum, column_u)
    column_sum = column_sum.reshape(-1, 2, ROW_DEV, LANES)
    return facet_rows(column_sum, table, column_u, n_local)


def solution(mesh):
    return jax.shard_map(
        local,
        mesh=mesh,
        in_specs=(
            P("sub", None, ("frow", "fcol"), None),
            P(("frow", "fcol"), None),
            P("sub"),
            P("sub"),
            P(),
        ),
        out_specs=P("fcol", None, ("sub", "frow"), None),
        check_vma=False,
    )
```
